768 devices in a mesh: grp: 96 (over y, z), sub: 8 (over x, core).
Axes of the slice: x: 4, y: 8, z: 12, core: 2. Of those that a mesh axis runs over, the one named last changes fastest.
Arguments:
- adjoint: float32 [5, 512, 98304], P(None, None, ('grp', 'sub')), may hold values from -15 to 15
- velocity: float32 [3, 512, 98304], P(None, None, ('grp', 'sub')), may hold values from -6 to 6
- geometry: float32 [4, 98304], P(None, ('grp', 'sub')), may hold values from 0.5 to 2
- face_codes: int32 [768, 704], P(('grp', 'sub')), may hold values from -1 to 767, as said below
Outputs:
- solution: float32 [5, 512, 98304], P(None, None, ('grp', 'sub'))
The draws below stay inside these ranges and needn't reach their ends.
Inputs may be any that keep to these rules, and one draw needn't show every extreme that they name: `face_codes`: on the device of group g and owner p, slots f and f + 288 of the first block are partners for f < 288, both empty or both live. Then block q holds slots f = 0..15: block p is empty; for q != p, slot f of block q and slot f of block p on the device of group g and owner q are partners and are both empty or both live. No face of an element is named twice in one device's list. In every group some pair of owners has all 16 slots of their blocks live.
All inputs are finite; a program needn't handle non-finite values.
Results may differ from the reference program's by a relative error of at most 0.00045.
Values sent between devices are 32-bit elements; how exact they have to be, the bound alone decides.
A program may use at most 64 MiB of HBM per device.

```python
import math
import jax
import jax.numpy as jnp
from jax import lax

COMP = 5
POINTS = 512
E_DEV = 128
ITERS = 2
LPAIR = 288
FMAX = 16
ELEMS = 98304
N_GRP = 96
N_SUB = 8
DEVICES = 768


def draw_adjoint(key, part):
    position = jnp.arange(ELEMS, dtype=jnp.float32) / max(ELEMS - 1, 1)
    base = jnp.clip(jax.random.normal(key, (COMP, POINTS, ELEMS), jnp.float32), -5.0, 5.0)
    scale = 1.0 + 2.0 * position
    return base * scale[None, None, :]


def draw_face_codes(key, part):
    owners = N_SUB
    face_total = 6 * E_DEV
    local_slots = 2 * LPAIR
    subkeys = jax.random.split(key, 4)
    scores = jax.random.randint(subkeys[0], (DEVICES, face_total), 0, 1 << 20) * face_total + jnp.arange(face_total)[None, :]
    shuffled = jnp.argsort(scores, axis=-1).astype(jnp.int32)
    local_ids = shuffled[:, :local_slots]
    peer_ids = shuffled[:, local_slots:local_slots + owners * FMAX].reshape(N_GRP, owners, owners, FMAX)
    local_count = jax.random.randint(subkeys[1], (DEVICES, 1), LPAIR // 2, LPAIR + 1)
    slot_index = jnp.arange(local_slots) % LPAIR
    local_live = slot_index[None, :] < local_count
    local_codes = jnp.where(local_live, local_ids, -1)
    counts = jax.random.randint(subkeys[2], (N_GRP, owners, owners), max(1, FMAX // 4), FMAX + 1)
    upper = jnp.triu(counts, 1)
    counts = upper + jnp.swapaxes(upper, 1, 2)
    chosen = jax.random.randint(subkeys[3], (N_GRP, 1, 1), 0, owners)
    partner = (chosen + 1) % owners
    rows = jnp.arange(owners)[None, :, None]
    cols = jnp.arange(owners)[None, None, :]
    forced = (rows == chosen) & (cols == partner) | (rows == partner) & (cols == chosen)
    counts = jnp.where(forced, FMAX, counts)
    peer_live = jnp.arange(FMAX)[None, None, None, :] < counts[..., None]
    peer_codes = jnp.where(peer_live, peer_ids, -1).reshape(DEVICES, owners * FMAX)
    return jnp.concatenate([local_codes, peer_codes], axis=1).astype(jnp.int32)


def levels(own_key, shape, shards, low, high):
    def one(dim, blocks):
        draws = jax.random.uniform(jax.random.fold_in(jax.random.fold_in(own_key, 6), dim), (blocks,), jnp.float32, low / len(shards), high / len(shards))
        return jnp.repeat(jnp.exp(draws), shape[dim] // blocks).reshape((-1,) + (1,) * (len(shape) - dim - 1))

    gain = one(*shards[0])
    for cut in shards[1:]:
        gain = gain * one(*cut)
    return gain


def normal_values(rng, dims, scale, reach, pieces=(), held_as=jnp.bfloat16):
    values = scale * jax.random.normal(rng, dims, jnp.float32)
    if pieces:
        values = values * levels(rng, dims, pieces, -0.22, 0.18)
    return jnp.clip(values, -reach, reach).astype(held_as)


def setup_inputs(seed: int = 0) -> dict:
    seeds = jax.random.split(jax.random.key(seed), 5)
    adjoint = draw_adjoint(jax.random.fold_in(seeds[4], 71), 0)
    velocity = normal_values(seeds[1], (3, POINTS, ELEMS), 1.0, 6.0, ((2, 768),), jnp.float32)
    geometry = jnp.clip(jnp.exp(math.log(2.0) - 1.3862944 * jax.random.uniform(seeds[2], (4, ELEMS), jnp.float32) ** levels(seeds[2], (4, ELEMS), ((1, 768),), -0.2, 0.2)), 0.5, 2.0)
    face_codes = draw_face_codes(jax.random.fold_in(seeds[4], 71), 0)
    return {"adjoint": adjoint, "velocity": velocity, "geometry": geometry, "face_codes": face_codes}


TIME_STEP = 0.05
DIFFUSIVITY = (1.0, 1.0, 1.0, 0.7, 0.2)
EINSUM_FORMS = ("ia,...ajke->...ijke", "ja,...iake->...ijke", "ka,...ijae->...ijke")
GLL_POINTS = (-1.0, -0.8717401485096066, -0.5917001814331423, -0.2092992179024789, 0.2092992179024789, 0.5917001814331423, 0.8717401485096066, 1.0)


def legendre_seven(point):
    before = 1.0
    current = point
    for order in range(1, 7):
        following = ((2 * order + 1) * point * current - order * before) / (order + 1)
        before = current
        current = following
    return current


def gll_tables():
    points = list(GLL_POINTS)
    values = [legendre_seven(point) for point in points]
    weights = [2.0 / (56.0 * value * value) for value in values]
    derivative = []
    for row_index in range(8):
        line = []
        for col_index in range(8):
            if row_index == col_index:
                line.append(0.0)
            else:
                line.append(values[row_index] / (values[col_index] * (points[row_index] - points[col_index])))
        derivative.append(line)
    derivative[0][0] = -14.0
    derivative[7][7] = 14.0
    weight_cube = []
    for row_index in range(8):
        for col_index in range(8):
            for depth_index in range(8):
                weight_cube.append(weights[row_index] * weights[col_index] * weights[depth_index])
    rows = []
    for face in range(6):
        direction = face // 2
        level = 7 * (face % 2)
        entries = []
        for first_pos in range(1, 7):
            for second_pos in range(1, 7):
                if direction == 0:
                    entries.append(level * 64 + first_pos * 8 + second_pos)
                elif direction == 1:
                    entries.append(first_pos * 64 + level * 8 + second_pos)
                else:
                    entries.append(first_pos * 64 + second_pos * 8 + level)
        rows.append(entries)
    return derivative, weight_cube, rows


def along(field, matrix, axis):
    shape = field.shape
    cube = field.reshape(shape[:-2] + (8, 8, 8, shape[-1]))
    result = jnp.einsum(EINSUM_FORMS[axis], matrix, cube, precision=lax.Precision.HIGHEST)
    return result.reshape(shape)


def forcing_term(field, velocity, mass, scales, derivative):
    total = field / TIME_STEP
    for axis in range(3):
        total = total + velocity[axis] * scales[axis] * along(field, derivative, axis)
    return mass * total


def stiffness(field, mass, scales, kappa, derivative):
    total = mass * field / TIME_STEP
    for axis in range(3):
        flux = mass * scales[axis] * scales[axis] * along(field, derivative, axis)
        total = total + kappa * along(flux, derivative.T, axis)
    return total


def assemble(field, face_codes, face_table):
    local_slots = 2 * LPAIR
    live = face_codes >= 0
    safe = jnp.where(live, face_codes, 0)
    target = jnp.where(live, face_codes, 6 * E_DEV)
    blocks = field.reshape(POINTS, DEVICES, E_DEV)
    faces = jnp.transpose(blocks[face_table], (1, 2, 0, 3)).reshape(36, DEVICES, 6 * E_DEV)
    sent = jnp.take_along_axis(faces, safe[None], axis=2) * live[None].astype(field.dtype)
    own_part = jnp.roll(sent[:, :, :local_slots], LPAIR, axis=2)
    peer_part = sent[:, :, local_slots:].reshape(36, N_GRP, N_SUB, N_SUB, FMAX)
    peer_part = jnp.swapaxes(peer_part, 2, 3).reshape(36, DEVICES, N_SUB * FMAX)
    received = jnp.concatenate([own_part, peer_part], axis=2)

    def add_device(values, spots):
        return jnp.zeros((36, 6 * E_DEV + 1), values.dtype).at[:, spots].add(values)

    added = jax.vmap(add_device, in_axes=(1, 0), out_axes=1)(received, target)
    added = added[:, :, :6 * E_DEV].reshape(36, DEVICES, 6, E_DEV)
    added = jnp.transpose(added, (2, 0, 1, 3)).reshape(216, DEVICES, E_DEV)
    blocks = blocks.at[face_table.reshape(216)].add(added)
    return blocks.reshape(POINTS, ELEMS)


def point_weight(face_codes, face_table, dtype):
    target = jnp.where(face_codes >= 0, face_codes, 6 * E_DEV)

    def marks_device(spots):
        return jnp.zeros((6 * E_DEV + 1,), dtype).at[spots].add(1.0)[:6 * E_DEV]

    marks = jax.vmap(marks_device)(target).reshape(DEVICES, 6, E_DEV)
    marks = jnp.transpose(marks, (1, 0, 2))
    face_weight = jnp.broadcast_to((1.0 / (1.0 + marks))[:, None], (6, 36, DEVICES, E_DEV)).reshape(216, DEVICES, E_DEV)
    weight = jnp.ones((POINTS, DEVICES, E_DEV), dtype).at[face_table.reshape(216)].set(face_weight)
    return weight.reshape(POINTS, ELEMS)


def reference(adjoint, velocity, geometry, face_codes):
    derivative_list, weight_list, table_list = gll_tables()
    derivative = jnp.asarray(derivative_list, jnp.float32)
    weight_cube = jnp.asarray(weight_list, jnp.float32)
    face_table = jnp.asarray(table_list, jnp.int32)
    mass = weight_cube[:, None] * geometry[0][None, :]
    scales = geometry[1:]
    weight = point_weight(face_codes, face_table, adjoint.dtype)
    kappas = jnp.asarray(DIFFUSIVITY[:COMP], jnp.float32)

    def inner(first, second):
        return jnp.sum(weight * first * second)

    def solve_one(inputs):
        field, kappa = inputs
        assembled = assemble(forcing_term(field, velocity, mass, scales, derivative), face_codes, face_table)
        solution = jnp.zeros_like(assembled)
        residual = assembled
        direction = assembled
        norm_now = inner(residual, residual)
        for step in range(ITERS):
            image = assemble(stiffness(direction, mass, scales, kappa, derivative), face_codes, face_table)
            alpha = norm_now / inner(direction, image)
            solution = solution + alpha * direction
            residual = residual - alpha * image
            if step + 1 < ITERS:
                norm_next = inner(residual, residual)
                direction = residual + (norm_next / norm_now) * direction
                norm_now = norm_next
        return solution

    return lax.map(solve_one, (adjoint, kappas))
```

```python
import functools

import jax
import jax.numpy as jnp
from jax import lax
from jax.experimental import pallas as pl
from jax.experimental.pallas import tpu as pltpu
from jax.sharding import PartitionSpec as P

MESH = pl.DeviceIdType.MESH
COMP = 5
POINTS = 512
LPAIR = 288
FMAX = 16
FACE_ROWS = 48
HALF_ROWS = 256
TIME_STEP = 0.05
DIFFUSIVITY = (1.0, 1.0, 1.0, 0.7, 0.2)
GLL_POINTS = (
    -1.0,
    -0.8717401485096066,
    -0.5917001814331423,
    -0.2092992179024789,
    0.2092992179024789,
    0.5917001814331423,
    0.8717401485096066,
    1.0,
)


def legendre_seven(point):
    before = 1.0
    current = point
    for order in range(1, 7):
        following = ((2 * order + 1) * point * current - order * before) / (order + 1)
        before = current
        current = following
    return current


def gll_tables():
    points = list(GLL_POINTS)
    values = [legendre_seven(point) for point in points]
    weights = [2.0 / (56.0 * value * value) for value in values]
    derivative = []
    for row in range(8):
        line = []
        for col in range(8):
            if row == col:
                line.append(0.0)
            else:
                line.append(values[row] / (values[col] * (points[row] - points[col])))
        derivative.append(line)
    derivative[0][0] = -14.0
    derivative[7][7] = 14.0
    stiffness = []
    for row in range(8):
        line = []
        for col in range(8):
            total = 0.0
            for mid in range(8):
                total += derivative[mid][row] * weights[mid] * derivative[mid][col]
            line.append(total / weights[row])
        stiffness.append(line)
    return weights, derivative, stiffness


def halves(matrix):
    even = [[0.5 * (matrix[i][a] + matrix[i][7 - a]) for a in range(4)] for i in range(4)]
    odd = [[0.5 * (matrix[i][a] - matrix[i][7 - a]) for a in range(4)] for i in range(4)]
    return even, odd


WEIGHTS, DERIVATIVE, STIFFNESS = gll_tables()
DERIVATIVE_HALVES = halves(DERIVATIVE) + (-1,)
STIFFNESS_HALVES = halves(STIFFNESS) + (1,)


def product(values, table):
    even, odd, sign = table
    sums = [values[a] + values[7 - a] for a in range(4)]
    gaps = [values[a] - values[7 - a] for a in range(4)]
    result = [None] * 8
    for i in range(4):
        first = sum(even[i][a] * sums[a] for a in range(1, 4)) + even[i][0] * sums[0]
        second = sum(odd[i][a] * gaps[a] for a in range(1, 4)) + odd[i][0] * gaps[0]
        result[i] = first + second
        result[7 - i] = first - second if sign > 0 else second - first
    return result


def rows(start):
    return pl.ds(pl.multiple_of(start, 8), 8)


def every_eighth(start):
    return pl.ds(start, 8, stride=8)


def sublane_sum(value):
    return jnp.sum(value, axis=0, keepdims=True)


def split(value):
    high = value.astype(jnp.bfloat16)
    low = (value - high.astype(jnp.float32)).astype(jnp.bfloat16)
    return high, low


def dot(first, second, dims):
    return lax.dot_general(
        first, second, (dims, ((), ())), preferred_element_type=jnp.float32
    )


def face_slice(face, base, step):
    direction, level = face // 2, 7 * (face % 2)
    if direction == 0:
        return pl.ds(pl.multiple_of(base + 64 * level + 8 * step, 8), 8)
    if direction == 1:
        return pl.ds(pl.multiple_of(base + 64 * step + 8 * level, 8), 8)
    return pl.ds(base + 64 * step + level, 8, stride=8)


def kernel(
    sizes,
    adjoint_hbm,
    velocity_hbm,
    geometry_hbm,
    codes_hbm,
    first_hbm,
    image_hbm,
    factor_ref,
    adjoint,
    velocity,
    geometry,
    codes,
    first,
    image,
    mass,
    along_i,
    along_k,
    columns,
    pairs,
    chosen,
    faces,
    gained,
    outgoing,
    incoming,
    partial,
    sub_slots,
    y_slots,
    z_slots,
    load_sem,
    store_sem,
    face_send,
    face_recv,
    sum_send,
    sum_recv,
):
    owners, n_y, n_z = sizes
    me = lax.axis_index("sub")
    group = lax.axis_index("grp")
    my_y = group // n_z
    my_z = group - my_y * n_z

    loads = [pltpu.make_async_copy(codes_hbm, codes, load_sem.at[0])]
    loads.append(pltpu.make_async_copy(geometry_hbm, geometry, load_sem.at[1]))
    loads.append(pltpu.make_async_copy(velocity_hbm, velocity, load_sem.at[2]))
    loads.append(pltpu.make_async_copy(adjoint_hbm, adjoint, load_sem.at[3]))
    for load in loads:
        load.start()

    barrier = pltpu.get_barrier_semaphore()

    def sub_peer(step):
        return lax.rem(me + step, owners)

    def y_peer(step):
        return lax.rem(my_y + step, n_y)

    def z_peer(step):
        return lax.rem(my_z + step, n_z)

    for step in range(1, owners):
        pl.semaphore_signal(barrier, inc=1, device_id={"sub": sub_peer(step)}, device_id_type=MESH)
    for step in range(1, n_y):
        pl.semaphore_signal(
            barrier, inc=1, device_id={"grp": y_peer(step) * n_z + my_z}, device_id_type=MESH
        )
    for step in range(1, n_z):
        pl.semaphore_signal(
            barrier, inc=1, device_id={"grp": my_y * n_z + z_peer(step)}, device_id_type=MESH
        )

    sublane = lax.broadcasted_iota(jnp.int32, (8, 128), 0)
    lane = lax.broadcasted_iota(jnp.int32, (8, 128), 1).astype(jnp.float32)
    inside = jnp.where((sublane >= 1) & (sublane <= 6), 1.0, 0.0)
    depth_weight = jnp.zeros((8, 128), jnp.float32)
    for k in range(8):
        depth_weight = jnp.where(sublane == k, WEIGHTS[k], depth_weight)

    loads[0].wait()
    for tile in range(6):
        width = min(128, 704 - 128 * tile)
        row = codes[:, 128 * tile : 128 * tile + width].astype(jnp.float32)
        columns[128 * tile : 128 * tile + width, :] = jnp.transpose(
            jnp.broadcast_to(row, (128, width))
        )

    def find(index, found):
        here = columns[rows(index * 8), :]
        there = columns[rows(index * 8 + LPAIR), :]
        result = []
        for face in range(6):
            place = lane + float(128 * face)
            result.append(
                found[face]
                + jnp.where(here == place, there + 1.0, 0.0)
                + jnp.where(there == place, here + 1.0, 0.0)
            )
        return tuple(result)

    found = lax.fori_loop(
        0, LPAIR // 8, find, tuple(jnp.zeros((8, 128), jnp.float32) for _ in range(6))
    )
    partner = [
        jnp.broadcast_to(sublane_sum(value) - 1.0, (16, 128)) for value in found
    ]
    row_id = lax.broadcasted_iota(jnp.int32, (16, 128), 0).astype(jnp.float32)

    def mark(index, carry):
        place = row_id + (index * 16).astype(jnp.float32)
        for face in range(6):
            pairs[pl.ds(pl.multiple_of(index * 16, 16), 16), 128 * face : 128 * face + 128] = (
                jnp.where(partner[face] == place, 1.0, 0.0).astype(jnp.bfloat16)
            )
        return carry

    lax.fori_loop(0, 48, mark, 0)
    lane16 = lax.broadcasted_iota(jnp.int32, (16, 128), 1).astype(jnp.float32)
    for block in range(owners):
        code = columns[2 * LPAIR + 16 * block : 2 * LPAIR + 16 * block + 16, :]
        for face in range(6):
            chosen[16 * block : 16 * block + 16, 128 * face : 128 * face + 128] = jnp.where(
                code == lane16 + float(128 * face), 1.0, 0.0
            ).astype(jnp.bfloat16)

    loads[1].wait()
    volume = jnp.broadcast_to(geometry[0:1, :], (8, 128))
    inverse = [jnp.broadcast_to(geometry[d : d + 1, :], (8, 128)) for d in range(1, 4)]
    squared = [value * value for value in inverse]
    weighted = volume * depth_weight
    for i in range(8):
        for j in range(8):
            mass[64 * i + 8 * j : 64 * i + 8 * j + 8, :] = weighted * (WEIGHTS[i] * WEIGHTS[j])
    loads[2].wait()

    def scale_velocity(index, carry):
        for d in range(3):
            place = rows(index * 8 + d * POINTS)
            velocity[place, :] = velocity[place, :] * inverse[d]
        return carry

    lax.fori_loop(0, 64, scale_velocity, 0, unroll=4)
    loads[3].wait()

    zero = jnp.zeros((8, 128), jnp.float32)

    def sweep(source, base, table, factors, finish):
        def lines(r, carry):
            values = [source[rows(base + 64 * i + 8 * r), :] for i in range(8)]
            moved = product(values, table)
            for i in range(8):
                along_i[rows(64 * i + 8 * r), :] = (
                    values[i] * (1.0 / TIME_STEP) + factors(0, 64 * i + 8 * r) * moved[i]
                )
            values = [source[every_eighth(base + 64 * r + k), :] for k in range(8)]
            moved = product(values, table)
            for k in range(8):
                along_k[every_eighth(64 * r + k), :] = moved[k]
            return carry

        lax.fori_loop(0, 8, lines, 0)

        def close(i, carry):
            values = [source[rows(base + 64 * i + 8 * j), :] for j in range(8)]
            moved = product(values, table)
            for j in range(8):
                place = 64 * i + 8 * j
                total = along_i[rows(place), :] + factors(1, place) * moved[j]
                total = total + factors(2, place) * along_k[rows(place), :]
                carry = finish(place, values[j], mass[rows(place), :] * total, carry)
            return carry

        return lax.fori_loop(0, 8, close, (zero, zero))

    def note(quantity, comp, value):
        partial[pl.ds(quantity * 8 + comp, 1), :] = sublane_sum(value)

    def force(comp, carry):
        base = pl.multiple_of(comp * POINTS, POINTS)

        def finish(place, value, total, sums):
            first[rows(base + place), :] = total
            return sums[0] + total * total, sums[1]

        sums = sweep(
            adjoint,
            base,
            DERIVATIVE_HALVES,
            lambda d, place: velocity[rows(d * POINTS + place), :],
            finish,
        )
        note(0, comp, sums[0])
        return carry

    def kappas(comp):
        kappa = jnp.where(comp == 3, DIFFUSIVITY[3], DIFFUSIVITY[0])
        kappa = jnp.where(comp == 4, DIFFUSIVITY[4], kappa)
        return [kappa * value for value in squared]

    def spread(comp, carry):
        base = pl.multiple_of(comp * POINTS, POINTS)
        scaled = kappas(comp)

        def finish(place, value, total, sums):
            image[rows(base + place), :] = total
            return sums[0] + value * total, sums[1] + total * total

        sums = sweep(first, base, STIFFNESS_HALVES, lambda d, place: scaled[d], finish)
        note(1, comp, sums[0])
        note(2, comp, sums[1])
        return carry

    def energy(comp, carry):
        base = pl.multiple_of(comp * POINTS, POINTS)
        scaled = kappas(comp)

        def finish(place, value, total, sums):
            return sums[0] + value * total, sums[1]

        sums = sweep(image, base, STIFFNESS_HALVES, lambda d, place: scaled[d], finish)
        note(3, comp, sums[0])
        return carry

    def face_copy(turn, step):
        peer = sub_peer(step)
        return pltpu.make_async_remote_copy(
            src_ref=outgoing.at[turn, pl.ds(pl.multiple_of(peer * FMAX, FMAX), FMAX)],
            dst_ref=incoming.at[turn, pl.ds(pl.multiple_of(me * FMAX, FMAX), FMAX)],
            send_sem=face_send.at[turn, step],
            recv_sem=face_recv.at[turn, step],
            device_id={"sub": peer},
            device_id_type=MESH,
        )

    def assemble(turn, field, quantity):
        def gather(comp, carry):
            base = pl.multiple_of(comp * POINTS, POINTS)
            top = pl.multiple_of(comp * FACE_ROWS, 16)
            for face in range(6):
                block = jnp.concatenate(
                    [field[face_slice(face, base, a), :] * inside for a in range(1, 7)], axis=0
                )
                high, low = split(block)
                place = slice(128 * face, 128 * face + 128)
                faces[pl.ds(top, FACE_ROWS), place] = high
                faces[pl.ds(pl.multiple_of(top + HALF_ROWS, 16), FACE_ROWS), place] = low
            return carry

        lax.fori_loop(0, COMP, gather, 0)
        over_lanes = ((1,), (1,))
        outgoing[turn] = dot(chosen[...], faces[0:HALF_ROWS, :], over_lanes) + dot(
            chosen[...], faces[HALF_ROWS:, :], over_lanes
        )
        incoming[turn, pl.ds(pl.multiple_of(me * FMAX, FMAX), FMAX), :] = jnp.zeros(
            (FMAX, HALF_ROWS), jnp.float32
        )
        if turn == 0:
            pl.semaphore_wait(barrier, owners - 1 + n_y - 1 + n_z - 1)
        copies = [face_copy(turn, step) for step in range(1, owners)]
        for copy in copies:
            copy.start()
        plain = ((1,), (0,))
        for part in range(3):
            place = slice(256 * part, 256 * part + 256)
            gained[:, place] = dot(faces[0:HALF_ROWS, :], pairs[:, place], plain) + dot(
                faces[HALF_ROWS:, :], pairs[:, place], plain
            )
        for copy in copies:
            copy.wait_recv()
        arrived = [
            split(jnp.transpose(incoming[turn, :, 128 * part : 128 * part + 128]))
            for part in range(2)
        ]
        for half in range(2):
            strip = slice(128 * half, 128 * half + 128)
            for part in range(3):
                place = slice(256 * part, 256 * part + 256)
                gained[strip, place] = (
                    gained[strip, place]
                    + dot(arrived[half][0], chosen[:, place], plain)
                    + dot(arrived[half][1], chosen[:, place], plain)
                )

        def add(comp, carry):
            base = pl.multiple_of(comp * POINTS, POINTS)
            sums = zero
            for face in range(6):
                for a in range(6):
                    place = face_slice(face, base, a + 1)
                    more = gained[rows(comp * FACE_ROWS + 8 * a), 128 * face : 128 * face + 128]
                    value = field[place, :]
                    sums = sums + value * more
                    field[place, :] = value + more
            here = pl.ds(quantity * 8 + comp, 1)
            partial[here, :] = partial[here, :] + sublane_sum(sums)
            return carry

        lax.fori_loop(0, COMP, add, 0)
        for copy in copies:
            copy.wait_send()

    faces[COMP * FACE_ROWS : HALF_ROWS, :] = jnp.zeros((16, 768), jnp.bfloat16)
    faces[HALF_ROWS + COMP * FACE_ROWS :, :] = jnp.zeros((16, 768), jnp.bfloat16)
    partial[...] = jnp.zeros((32, 128), jnp.float32)

    lax.fori_loop(0, COMP, force, 0)
    assemble(0, first, 0)
    save_first = pltpu.make_async_copy(first, first_hbm, store_sem.at[0])
    save_first.start()
    lax.fori_loop(0, COMP, spread, 0)
    assemble(1, image, 2)
    save_image = pltpu.make_async_copy(image, image_hbm, store_sem.at[1])
    save_image.start()
    lax.fori_loop(0, COMP, energy, 0)

    entry = lax.broadcasted_iota(jnp.int32, (32, 128), 0)
    column = lax.broadcasted_iota(jnp.int32, (32, 128), 1)
    diagonal = entry == column
    whole = jnp.sum(partial[...], axis=1, keepdims=True)
    row = jnp.sum(jnp.where(diagonal, whole, 0.0), axis=0, keepdims=True)

    def total(row, slots, count, mine, peer, target, offset):
        slots[mine] = row
        copies = []
        for step in range(1, count):
            copies.append(
                pltpu.make_async_remote_copy(
                    src_ref=slots.at[mine],
                    dst_ref=slots.at[mine],
                    send_sem=sum_send.at[offset + step],
                    recv_sem=sum_recv.at[offset + step],
                    device_id=target(peer(step)),
                    device_id_type=MESH,
                )
            )
        for copy in copies:
            copy.start()
        for copy in copies:
            copy.wait_recv()
        result = jnp.sum(slots[...], axis=0)
        return result, copies

    row, sent_sub = total(row, sub_slots, owners, me, sub_peer, lambda p: {"sub": p}, 0)
    row, sent_y = total(
        row, y_slots, n_y, my_y, y_peer, lambda p: {"grp": p * n_z + my_z}, owners
    )
    row, sent_z = total(
        row, z_slots, n_z, my_z, z_peer, lambda p: {"grp": my_y * n_z + p}, owners + n_y
    )
    spreaded = jnp.where(diagonal, jnp.broadcast_to(row, (32, 128)), 0.0)
    totals = jnp.broadcast_to(jnp.sum(spreaded, axis=1, keepdims=True), (32, 128))
    bb, bq, qq, qhq = (totals[8 * n : 8 * n + 8] for n in range(4))
    alpha = bb / bq
    scaled_qq = alpha * qq
    norm_next = alpha * scaled_qq - bb
    beta = norm_next / bb
    up = 1.0 + beta
    curve = up * (up * bq - 2.0 * scaled_qq) + alpha * (alpha * qhq)
    alpha_next = norm_next / curve
    factor_ref[0:8, :] = alpha + alpha_next * up
    factor_ref[8:16, :] = -alpha * alpha_next
    for copy in sent_sub + sent_y + sent_z:
        copy.wait_send()
    save_first.wait()
    save_image.wait()


def solution(mesh):
    owners, groups = mesh.shape["sub"], mesh.shape["grp"]
    n_z = 12 if groups % 12 == 0 else max(1, groups // 2)
    n_y = groups // n_z

    def shards(adjoint, velocity, geometry, face_codes):
        elements = adjoint.shape[2]
        flat = COMP * POINTS
        vmem = pltpu.VMEM
        f32, bf16 = jnp.float32, jnp.bfloat16
        anywhere = pl.BlockSpec(memory_space=pl.ANY)
        first, image, factor = pl.pallas_call(
            functools.partial(kernel, (owners, n_y, n_z)),
            out_shape=(
                jax.ShapeDtypeStruct((flat, elements), f32),
                jax.ShapeDtypeStruct((flat, elements), f32),
                jax.ShapeDtypeStruct((16, elements), f32),
            ),
            in_specs=[anywhere] * 4,
            out_specs=(anywhere, anywhere, pl.BlockSpec(memory_space=pltpu.VMEM)),
            scratch_shapes=[
                vmem((flat, elements), f32),
                vmem((3 * POINTS, elements), f32),
                vmem((4, elements), f32),
                vmem((1, 704), jnp.int32),
                vmem((flat, elements), f32),
                vmem((flat, elements), f32),
                vmem((POINTS, elements), f32),
                vmem((POINTS, elements), f32),
                vmem((POINTS, elements), f32),
                vmem((704, 128), f32),
                vmem((768, 768), bf16),
                vmem((128, 768), bf16),
                vmem((2 * HALF_ROWS, 768), bf16),
                vmem((HALF_ROWS, 768), f32),
                vmem((2, 128, HALF_ROWS), f32),
                vmem((2, 128, HALF_ROWS), f32),
                vmem((32, 128), f32),
                vmem((owners, 1, 128), f32),
                vmem((n_y, 1, 128), f32),
                vmem((n_z, 1, 128), f32),
                pltpu.SemaphoreType.DMA((4,)),
                pltpu.SemaphoreType.DMA((2,)),
                pltpu.SemaphoreType.DMA((2, owners)),
                pltpu.SemaphoreType.DMA((2, owners)),
                pltpu.SemaphoreType.DMA((owners + n_y + n_z,)),
                pltpu.SemaphoreType.DMA((owners + n_y + n_z,)),
            ],
            compiler_params=pltpu.CompilerParams(
                collective_id=0, has_side_effects=True, vmem_limit_bytes=32 * 1024 * 1024
            ),
        )(
            adjoint.reshape(flat, elements),
            velocity.reshape(3 * POINTS, elements),
            geometry,
            face_codes,
        )
        shape = (COMP, POINTS, elements)
        return (
            factor[0:COMP, None, :] * first.reshape(shape)
            + factor[8 : 8 + COMP, None, :] * image.reshape(shape)
        )

    placed = (
        P(None, None, ("grp", "sub")),
        P(None, None, ("grp", "sub")),
        P(None, ("grp", "sub")),
        P(("grp", "sub"), None),
    )
    return jax.shard_map(
        shards, mesh=mesh, in_specs=placed, out_specs=P(None, None, ("grp", "sub")), check_vma=False
    )
```

```python
import functools

import jax
import jax.numpy as jnp
from jax import lax
from jax.experimental import pallas as pl
from jax.experimental.pallas import tpu as pltpu
from jax.sharding import PartitionSpec as P

MESH = pl.DeviceIdType.MESH
COMP = 5
POINTS = 512
LPAIR = 288
FMAX = 16
FACE_ROWS = 48
HALF_ROWS = 256
TIME_STEP = 0.05
DIFFUSIVITY = (1.0, 1.0, 1.0, 0.7, 0.2)
GLL_POINTS = (
    -1.0,
    -0.8717401485096066,
    -0.5917001814331423,
    -0.2092992179024789,
    0.2092992179024789,
    0.5917001814331423,
    0.8717401485096066,
    1.0,
)


def legendre_seven(point):
    before = 1.0
    current = point
    for order in range(1, 7):
        following = ((2 * order + 1) * point * current - order * before) / (order + 1)
        before = current
        current = following
    return current


def gll_tables():
    points = list(GLL_POINTS)
    values = [legendre_seven(point) for point in points]
    weights = [2.0 / (56.0 * value * value) for value in values]
    derivative = []
    for row in range(8):
        line = []
        for col in range(8):
            if row == col:
                line.append(0.0)
            else:
                line.append(values[row] / (values[col] * (points[row] - points[col])))
        derivative.append(line)
    derivative[0][0] = -14.0
    derivative[7][7] = 14.0
    stiffness = []
    for row in range(8):
        line = []
        for col in range(8):
            total = 0.0
            for mid in range(8):
                total += derivative[mid][row] * weights[mid] * derivative[mid][col]
            line.append(total / weights[row])
        stiffness.append(line)
    return weights, derivative, stiffness


def halves(matrix):
    even = [[0.5 * (matrix[i][a] + matrix[i][7 - a]) for a in range(4)] for i in range(4)]
    odd = [[0.5 * (matrix[i][a] - matrix[i][7 - a]) for a in range(4)] for i in range(4)]
    return even, odd


def triangle(matrix):
    result = [[0.0] * 4 for _ in range(4)]
    for r in range(4):
        pivot = matrix[r][r] - sum(result[m][r] ** 2 for m in range(r))
        if pivot < 1e-9 * matrix[r][r]:
            continue
        result[r][r] = pivot**0.5
        for c in range(r + 1, 4):
            rest = matrix[r][c] - sum(result[m][r] * result[m][c] for m in range(r))
            result[r][c] = rest / result[r][r]
    return result


WEIGHTS, DERIVATIVE, STIFFNESS = gll_tables()
SYMMETRIC_HALVES = halves([[WEIGHTS[i] * v for v in STIFFNESS[i]] for i in range(8)])
SQUARES = tuple(triangle(part) for part in SYMMETRIC_HALVES)
GROUPS = ((0, 2), (2, 4), (4, 5))
DERIVATIVE_HALVES = halves(DERIVATIVE) + (-1,)
STIFFNESS_HALVES = halves(STIFFNESS) + (1,)


def product(values, table):
    even, odd, sign = table
    sums = [values[a] + values[7 - a] for a in range(4)]
    gaps = [values[a] - values[7 - a] for a in range(4)]
    result = [None] * 8
    for i in range(4):
        first = sum(even[i][a] * sums[a] for a in range(1, 4)) + even[i][0] * sums[0]
        second = sum(odd[i][a] * gaps[a] for a in range(1, 4)) + odd[i][0] * gaps[0]
        result[i] = first + second
        result[7 - i] = first - second if sign > 0 else second - first
    return result


def quadratic(values):
    sums = [values[a] + values[7 - a] for a in range(4)]
    gaps = [values[a] - values[7 - a] for a in range(4)]
    result = None
    for table, part in zip(SQUARES, (sums, gaps)):
        for r in range(4):
            if table[r][r] == 0.0:
                continue
            term = table[r][r] * part[r]
            for c in range(r + 1, 4):
                term = term + table[r][c] * part[c]
            term = term * term
            result = term if result is None else result + term
    return result


def rows(start):
    return pl.ds(pl.multiple_of(start, 8), 8)


def every_eighth(start):
    return pl.ds(start, 8, stride=8)


def sublane_sum(value):
    return jnp.sum(value, axis=0, keepdims=True)


def split(value):
    high = value.astype(jnp.bfloat16)
    low = (value - high.astype(jnp.float32)).astype(jnp.bfloat16)
    return high, low


def dot(first, second, dims):
    return lax.dot_general(
        first, second, (dims, ((), ())), preferred_element_type=jnp.float32
    )


def face_slice(face, base, step):
    direction, level = face // 2, 7 * (face % 2)
    if direction == 0:
        return pl.ds(pl.multiple_of(base + 64 * level + 8 * step, 8), 8)
    if direction == 1:
        return pl.ds(pl.multiple_of(base + 64 * step + 8 * level, 8), 8)
    return pl.ds(base + 64 * step + level, 8, stride=8)


def kernel(
    sizes,
    adjoint_hbm,
    velocity_hbm,
    geometry_hbm,
    codes_hbm,
    first,
    image,
    factor_ref,
    adjoint,
    velocity,
    geometry,
    codes,
    mass,
    along_i,
    along_k,
    columns,
    pairs,
    chosen,
    faces,
    gained,
    outgoing,
    incoming,
    partial,
    near_slots,
    far_slots,
    load_sem,
    face_send,
    face_recv,
    near_send,
    near_recv,
    far_send,
    far_recv,
):
    owners, n_y, n_z = sizes
    n_x = owners // 2
    me = lax.axis_index("sub")
    group = lax.axis_index("grp")
    my_y = group // n_z
    my_z = group - my_y * n_z
    my_x = me // 2
    my_core = me - my_x * 2

    def load(index, source, target):
        return pltpu.make_async_copy(source, target, load_sem.at[index])

    loads = [load(0, codes_hbm, codes), load(1, geometry_hbm, geometry)]
    loads.append(load(2, velocity_hbm, velocity))
    for index, (low, high) in enumerate(GROUPS):
        part = pl.ds(low * POINTS, (high - low) * POINTS)
        loads.append(load(3 + index, adjoint_hbm.at[part], adjoint.at[part]))
    for copy in loads:
        copy.start()

    barrier = pltpu.get_barrier_semaphore()
    n_near, n_far = 2 * n_z, n_x * n_y
    near_me = my_z * 2 + my_core
    far_me = my_y * n_x + my_x

    def sub_peer(step):
        return {"grp": group, "sub": lax.rem(me + step, owners)}

    def near_peer(step):
        place = lax.rem(near_me + step, n_near)
        z = place // 2
        return {"grp": my_y * n_z + z, "sub": my_x * 2 + (place - z * 2)}

    def far_peer(step):
        place = lax.rem(far_me + step, n_far)
        y = place // n_x
        return {"grp": y * n_z + my_z, "sub": (place - y * n_x) * 2 + my_core}

    for count, peer in ((owners, sub_peer), (n_near, near_peer), (n_far, far_peer)):

        def greet(step, carry, peer=peer):
            pl.semaphore_signal(barrier, inc=1, device_id=peer(step), device_id_type=MESH)
            return carry

        lax.fori_loop(1, count, greet, 0)

    sublane = lax.broadcasted_iota(jnp.int32, (8, 128), 0)
    lane = lax.broadcasted_iota(jnp.int32, (8, 128), 1).astype(jnp.float32)
    inside = jnp.where((sublane >= 1) & (sublane <= 6), 1.0, 0.0)
    depth_weight = jnp.zeros((8, 128), jnp.float32)
    for k in range(8):
        depth_weight = jnp.where(sublane == k, WEIGHTS[k], depth_weight)
    zero = jnp.zeros((8, 128), jnp.float32)

    loads[0].wait()
    for tile in range(6):
        width = min(128, 704 - 128 * tile)
        row = codes[:, 128 * tile : 128 * tile + width].astype(jnp.float32)
        columns[128 * tile : 128 * tile + width, :] = jnp.transpose(
            jnp.broadcast_to(row, (128, width))
        )
    lane16 = lax.broadcasted_iota(jnp.int32, (16, 128), 1).astype(jnp.float32)
    for block in range(owners):
        code = columns[2 * LPAIR + 16 * block : 2 * LPAIR + 16 * block + 16, :]
        for face in range(6):
            chosen[16 * block : 16 * block + 16, 128 * face : 128 * face + 128] = jnp.where(
                code == lane16 + float(128 * face), 1.0, 0.0
            ).astype(jnp.bfloat16)
    for turn in range(2):
        own = pl.ds(pl.multiple_of(me * FMAX, FMAX), FMAX)
        for index in range(len(GROUPS)):
            outgoing[turn, index, :, 96:128] = jnp.zeros((128, 32), jnp.float32)
            incoming[turn, index, own, :] = jnp.zeros((FMAX, 128), jnp.float32)
    outgoing[:, 2, :, 0:128] = jnp.zeros((2, 128, 128), jnp.float32)

    loads[1].wait()
    volume = jnp.broadcast_to(geometry[0:1, :], (8, 128))
    inverse = [jnp.broadcast_to(geometry[d : d + 1, :], (8, 128)) for d in range(1, 4)]
    squared = [value * value for value in inverse]
    weighted = volume * depth_weight
    for i in range(8):
        for j in range(8):
            mass[64 * i + 8 * j : 64 * i + 8 * j + 8, :] = weighted * (WEIGHTS[i] * WEIGHTS[j])
    loads[2].wait()

    def scale_velocity(index, carry):
        for d in range(3):
            place = rows(index * 8 + d * POINTS)
            velocity[place, :] = velocity[place, :] * inverse[d]
        return carry

    lax.fori_loop(0, 64, scale_velocity, 0, unroll=4)

    def build_pairs():
        def find(index, found):
            here = columns[rows(index * 8), :]
            there = columns[rows(index * 8 + LPAIR), :]
            result = []
            for face in range(6):
                place = lane + float(128 * face)
                result.append(
                    found[face]
                    + jnp.where(here == place, there + 1.0, 0.0)
                    + jnp.where(there == place, here + 1.0, 0.0)
                )
            return tuple(result)

        found = lax.fori_loop(0, LPAIR // 8, find, (zero,) * 6, unroll=4)
        partner = [jnp.broadcast_to(sublane_sum(value) - 1.0, (16, 128)) for value in found]
        row_id = lax.broadcasted_iota(jnp.int32, (16, 128), 0).astype(jnp.float32)

        def mark(index, carry):
            place = row_id + (index * 16).astype(jnp.float32)
            here = pl.ds(pl.multiple_of(index * 16, 16), 16)
            for face in range(6):
                pairs[here, 128 * face : 128 * face + 128] = jnp.where(
                    partner[face] == place, 1.0, 0.0
                ).astype(jnp.bfloat16)
            return carry

        lax.fori_loop(0, 48, mark, 0, unroll=2)

    def sweep(source, base, table, factors, finish):
        def lines(r, carry):
            values = [source[rows(base + 64 * i + 8 * r), :] for i in range(8)]
            moved = product(values, table)
            for i in range(8):
                along_i[rows(64 * i + 8 * r), :] = (
                    values[i] * (1.0 / TIME_STEP) + factors(0, 64 * i + 8 * r) * moved[i]
                )
            values = [source[every_eighth(base + 64 * r + k), :] for k in range(8)]
            moved = product(values, table)
            for k in range(8):
                along_k[every_eighth(64 * r + k), :] = moved[k]
            return carry

        lax.fori_loop(0, 8, lines, 0)

        def close(i, carry):
            values = [source[rows(base + 64 * i + 8 * j), :] for j in range(8)]
            moved = product(values, table)
            for j in range(8):
                place = 64 * i + 8 * j
                total = along_i[rows(place), :] + factors(1, place) * moved[j]
                total = total + factors(2, place) * along_k[rows(place), :]
                carry = finish(place, values[j], mass[rows(place), :] * total, carry)
            return carry

        return lax.fori_loop(0, 8, close, (zero, zero))

    def note(quantity, comp, value):
        partial[pl.ds(quantity * 8 + comp, 1), :] = sublane_sum(value)

    def force(comp, carry):
        base = pl.multiple_of(comp * POINTS, POINTS)

        def finish(place, value, total, sums):
            first[rows(base + place), :] = total
            return sums[0] + total * total, sums[1]

        sums = sweep(
            adjoint,
            base,
            DERIVATIVE_HALVES,
            lambda d, place: velocity[rows(d * POINTS + place), :],
            finish,
        )
        note(0, comp, sums[0])
        return carry

    def kappas(comp):
        kappa = jnp.where(comp == 3, DIFFUSIVITY[3], DIFFUSIVITY[0])
        kappa = jnp.where(comp == 4, DIFFUSIVITY[4], kappa)
        return [kappa * value for value in squared]

    def spread(comp, carry):
        base = pl.multiple_of(comp * POINTS, POINTS)
        scaled = kappas(comp)

        def finish(place, value, total, sums):
            image[rows(base + place), :] = total
            return sums[0] + value * total, sums[1] + total * total

        sums = sweep(first, base, STIFFNESS_HALVES, lambda d, place: scaled[d], finish)
        note(1, comp, sums[0])
        note(2, comp, sums[1])
        return carry

    def energy(comp, carry):
        base = pl.multiple_of(comp * POINTS, POINTS)
        scaled = kappas(comp)
        forms = [zero, zero, zero]
        plain = zero
        for r in range(8):
            lines_i = [image[rows(base + 64 * i + 8 * r), :] for i in range(8)]
            forms[0] = forms[0] + WEIGHTS[r] * quadratic(lines_i)
            lines_j = [image[rows(base + 64 * r + 8 * j), :] for j in range(8)]
            forms[1] = forms[1] + WEIGHTS[r] * quadratic(lines_j)
            lines_k = [image[every_eighth(base + 64 * r + k), :] for k in range(8)]
            forms[2] = forms[2] + WEIGHTS[r] * quadratic(lines_k)
            level = [lines_j[j] * lines_j[j] for j in range(8)]
            level = sum((WEIGHTS[j] * (level[j] + level[7 - j]) for j in range(1, 4)), WEIGHTS[0] * (level[0] + level[7]))
            plain = plain + WEIGHTS[r] * level
        total = plain * (1.0 / TIME_STEP)
        for d in range(3):
            total = total + scaled[d] * forms[d]
        note(3, comp, weighted * total)
        return carry

    def face_copy(turn, index, step):
        peer = sub_peer(step)
        return pltpu.make_async_remote_copy(
            src_ref=outgoing.at[turn, index, pl.ds(pl.multiple_of(peer["sub"] * FMAX, FMAX), FMAX)],
            dst_ref=incoming.at[turn, index, pl.ds(pl.multiple_of(me * FMAX, FMAX), FMAX)],
            send_sem=face_send.at[turn, index, step],
            recv_sem=face_recv.at[turn, index, step],
            device_id=peer,
            device_id_type=MESH,
        )

    def each_copy(turn, index, act):
        def one(step, carry):
            act(face_copy(turn, index, step))
            return carry

        lax.fori_loop(1, owners, one, 0)

    def send(turn, index, field):
        low, high = GROUPS[index]

        def gather(comp, carry):
            base = pl.multiple_of(comp * POINTS, POINTS)
            top = pl.multiple_of(comp * FACE_ROWS, 16)
            for face in range(6):
                block = jnp.concatenate(
                    [field[face_slice(face, base, a), :] * inside for a in range(1, 7)], axis=0
                )
                big, small = split(block)
                place = slice(128 * face, 128 * face + 128)
                faces[pl.ds(top, FACE_ROWS), place] = big
                faces[pl.ds(pl.multiple_of(top + HALF_ROWS, 16), FACE_ROWS), place] = small
            return carry

        lax.fori_loop(low, high, gather, 0)
        start, stop = low * FACE_ROWS, high * FACE_ROWS
        over_lanes = ((1,), (1,))
        outgoing[turn, index, :, 0 : stop - start] = dot(
            chosen[...], faces[start:stop, :], over_lanes
        ) + dot(chosen[...], faces[HALF_ROWS + start : HALF_ROWS + stop, :], over_lanes)
        if turn == 0 and index == 0:
            pl.semaphore_wait(barrier, owners - 1 + n_near - 1 + n_far - 1)
        each_copy(turn, index, lambda copy: copy.start())

    plain_dims = ((1,), (0,))

    def local():
        for part in range(3):
            place = slice(256 * part, 256 * part + 256)
            gained[:, place] = dot(faces[0:HALF_ROWS, :], pairs[:, place], plain_dims) + dot(
                faces[HALF_ROWS:, :], pairs[:, place], plain_dims
            )

    def receive(turn, index, field, quantity):
        low, high = GROUPS[index]
        start, stop = low * FACE_ROWS, high * FACE_ROWS
        each_copy(turn, index, lambda copy: copy.wait_recv())
        big, small = split(jnp.transpose(incoming[turn, index])[0 : stop - start, :])
        for part in range(3):
            place = slice(256 * part, 256 * part + 256)
            gained[start:stop, place] = (
                gained[start:stop, place]
                + dot(big, chosen[:, place], plain_dims)
                + dot(small, chosen[:, place], plain_dims)
            )

        def add(comp, carry):
            base = pl.multiple_of(comp * POINTS, POINTS)
            sums = zero
            for face in range(6):
                for a in range(6):
                    place = face_slice(face, base, a + 1)
                    more = gained[rows(comp * FACE_ROWS + 8 * a), 128 * face : 128 * face + 128]
                    value = field[place, :]
                    sums = sums + value * more
                    field[place, :] = value + more
            here = pl.ds(quantity * 8 + comp, 1)
            partial[here, :] = partial[here, :] + sublane_sum(sums)
            return carry

        lax.fori_loop(low, high, add, 0)

    faces[COMP * FACE_ROWS : HALF_ROWS, :] = jnp.zeros((16, 768), jnp.bfloat16)
    faces[HALF_ROWS + COMP * FACE_ROWS :, :] = jnp.zeros((16, 768), jnp.bfloat16)
    partial[...] = jnp.zeros((32, 128), jnp.float32)

    for index, (low, high) in enumerate(GROUPS):
        loads[3 + index].wait()
        lax.fori_loop(low, high, force, 0)
        send(0, index, first)
    build_pairs()
    local()
    for index, (low, high) in enumerate(GROUPS):
        receive(0, index, first, 0)
        lax.fori_loop(low, high, spread, 0)
        send(1, index, image)
    local()
    for index, (low, high) in enumerate(GROUPS):
        receive(1, index, image, 2)
        lax.fori_loop(low, high, energy, 0)

    entry = lax.broadcasted_iota(jnp.int32, (32, 128), 0)
    column = lax.broadcasted_iota(jnp.int32, (32, 128), 1)
    diagonal = entry == column
    whole = jnp.sum(partial[...], axis=1, keepdims=True)
    row = jnp.sum(jnp.where(diagonal, whole, 0.0), axis=0, keepdims=True)

    def sum_copy(slots, mine, peer, send_sems, recv_sems, step):
        return pltpu.make_async_remote_copy(
            src_ref=slots.at[mine],
            dst_ref=slots.at[mine],
            send_sem=send_sems.at[step],
            recv_sem=recv_sems.at[step],
            device_id=peer(step),
            device_id_type=MESH,
        )

    stages = (
        (near_slots, n_near, near_me, near_peer, near_send, near_recv),
        (far_slots, n_far, far_me, far_peer, far_send, far_recv),
    )
    for slots, count, mine, peer, send_sems, recv_sems in stages:
        slots[mine] = row

        def begin(step, carry, given=(slots, mine, peer, send_sems, recv_sems)):
            sum_copy(*given, step).start()
            return carry

        def arrive(step, carry, given=(slots, mine, peer, send_sems, recv_sems)):
            sum_copy(*given, step).wait_recv()
            return carry

        lax.fori_loop(1, count, begin, 0)
        lax.fori_loop(1, count, arrive, 0)
        row = jnp.sum(slots[...], axis=0)

    spreaded = jnp.where(diagonal, jnp.broadcast_to(row, (32, 128)), 0.0)
    totals = jnp.broadcast_to(jnp.sum(spreaded, axis=1, keepdims=True), (32, 128))
    bb, bq, qq, qhq = (totals[8 * n : 8 * n + 8] for n in range(4))
    alpha = bb / bq
    scaled_qq = alpha * qq
    norm_next = alpha * scaled_qq - bb
    beta = norm_next / bb
    up = 1.0 + beta
    curve = up * (up * bq - 2.0 * scaled_qq) + alpha * (alpha * qhq)
    alpha_next = norm_next / curve
    factor_ref[0:8, :] = alpha + alpha_next * up
    factor_ref[8:16, :] = -alpha * alpha_next

    for turn in range(2):
        for index in range(len(GROUPS)):
            each_copy(turn, index, lambda copy: copy.wait_send())
    for slots, count, mine, peer, send_sems, recv_sems in stages:

        def leave(step, carry, given=(slots, mine, peer, send_sems, recv_sems)):
            sum_copy(*given, step).wait_send()
            return carry

        lax.fori_loop(1, count, leave, 0)


def solution(mesh):
    owners, groups = mesh.shape["sub"], mesh.shape["grp"]
    n_z = 12 if groups % 12 == 0 else max(1, groups // 2)
    n_y = groups // n_z

    def shards(adjoint, velocity, geometry, face_codes):
        elements = adjoint.shape[2]
        flat = COMP * POINTS
        vmem = pltpu.VMEM
        f32, bf16 = jnp.float32, jnp.bfloat16
        hbm = pl.BlockSpec(memory_space=pltpu.HBM)

        def keep(array):
            return pltpu.with_memory_space_constraint(array, pltpu.HBM)

        inner = pl.BlockSpec(memory_space=pltpu.VMEM)
        n_near, n_far = 2 * n_z, n_y * owners // 2
        dma = pltpu.SemaphoreType.DMA
        first, image, factor = pl.pallas_call(
            functools.partial(kernel, (owners, n_y, n_z)),
            out_shape=(
                pltpu.VMEM((flat, elements), f32),
                pltpu.VMEM((flat, elements), f32),
                pltpu.VMEM((16, elements), f32),
            ),
            in_specs=[hbm] * 4,
            out_specs=(inner, inner, inner),
            scratch_shapes=[
                vmem((flat, elements), f32),
                vmem((3 * POINTS, elements), f32),
                vmem((4, elements), f32),
                vmem((1, 704), jnp.int32),
                vmem((POINTS, elements), f32),
                vmem((POINTS, elements), f32),
                vmem((POINTS, elements), f32),
                vmem((704, 128), f32),
                vmem((768, 768), bf16),
                vmem((128, 768), bf16),
                vmem((2 * HALF_ROWS, 768), bf16),
                vmem((HALF_ROWS, 768), f32),
                vmem((2, len(GROUPS), 128, 128), f32),
                vmem((2, len(GROUPS), 128, 128), f32),
                vmem((32, 128), f32),
                vmem((n_near, 1, 128), f32),
                vmem((n_far, 1, 128), f32),
                dma((3 + len(GROUPS),)),
                dma((2, len(GROUPS), owners)),
                dma((2, len(GROUPS), owners)),
                dma((n_near,)),
                dma((n_near,)),
                dma((n_far,)),
                dma((n_far,)),
            ],
            compiler_params=pltpu.CompilerParams(
                collective_id=0, has_side_effects=True, vmem_limit_bytes=32 * 1024 * 1024
            ),
        )(
            keep(adjoint.reshape(flat, elements)),
            keep(velocity.reshape(3 * POINTS, elements)),
            keep(geometry),
            keep(face_codes),
        )
        shape = (COMP, POINTS, elements)
        return (
            factor[0:COMP, None, :] * first.reshape(shape)
            + factor[8 : 8 + COMP, None, :] * image.reshape(shape)
        )

    placed = (
        P(None, None, ("grp", "sub")),
        P(None, None, ("grp", "sub")),
        P(None, ("grp", "sub")),
        P(("grp", "sub"), None),
    )
    return jax.shard_map(
        shards, mesh=mesh, in_specs=placed, out_specs=P(None, None, ("grp", "sub")), check_vma=False
    )
```

```python
import functools

import jax
import jax.numpy as jnp
from jax import lax
from jax.experimental import pallas as pl
from jax.experimental.pallas import tpu as pltpu
from jax.sharding import PartitionSpec as P

MESH = pl.DeviceIdType.MESH
COMP = 5
POINTS = 512
LPAIR = 288
FMAX = 16
FACE_ROWS = 48
HALF_ROWS = 256
TIME_STEP = 0.05
DIFFUSIVITY = (1.0, 1.0, 1.0, 0.7, 0.2)
GLL_POINTS = (
    -1.0,
    -0.8717401485096066,
    -0.5917001814331423,
    -0.2092992179024789,
    0.2092992179024789,
    0.5917001814331423,
    0.8717401485096066,
    1.0,
)


def legendre_seven(point):
    before = 1.0
    current = point
    for order in range(1, 7):
        following = ((2 * order + 1) * point * current - order * before) / (order + 1)
        before = current
        current = following
    return current


def gll_tables():
    points = list(GLL_POINTS)
    values = [legendre_seven(point) for point in points]
    weights = [2.0 / (56.0 * value * value) for value in values]
    derivative = []
    for row in range(8):
        line = []
        for col in range(8):
            if row == col:
                line.append(0.0)
            else:
                line.append(values[row] / (values[col] * (points[row] - points[col])))
        derivative.append(line)
    derivative[0][0] = -14.0
    derivative[7][7] = 14.0
    stiffness = []
    for row in range(8):
        line = []
        for col in range(8):
            total = 0.0
            for mid in range(8):
                total += derivative[mid][row] * weights[mid] * derivative[mid][col]
            line.append(total / weights[row])
        stiffness.append(line)
    return weights, derivative, stiffness


def halves(matrix):
    even = [[0.5 * (matrix[i][a] + matrix[i][7 - a]) for a in range(4)] for i in range(4)]
    odd = [[0.5 * (matrix[i][a] - matrix[i][7 - a]) for a in range(4)] for i in range(4)]
    return even, odd


def triangle(matrix):
    result = [[0.0] * 4 for _ in range(4)]
    for r in range(4):
        pivot = matrix[r][r] - sum(result[m][r] ** 2 for m in range(r))
        if pivot < 1e-9 * matrix[r][r]:
            continue
        result[r][r] = pivot**0.5
        for c in range(r + 1, 4):
            rest = matrix[r][c] - sum(result[m][r] * result[m][c] for m in range(r))
            result[r][c] = rest / result[r][r]
    return result


WEIGHTS, DERIVATIVE, STIFFNESS = gll_tables()
SYMMETRIC_HALVES = halves([[WEIGHTS[i] * v for v in STIFFNESS[i]] for i in range(8)])
SQUARES = tuple(triangle(part) for part in SYMMETRIC_HALVES)
GROUPS = ((0, 2), (2, 4), (4, 5))
DERIVATIVE_HALVES = halves(DERIVATIVE) + (-1,)
STIFFNESS_HALVES = halves(STIFFNESS) + (1,)


def product(values, table):
    even, odd, sign = table
    sums = [values[a] + values[7 - a] for a in range(4)]
    gaps = [values[a] - values[7 - a] for a in range(4)]
    result = [None] * 8
    for i in range(4):
        first = sum(even[i][a] * sums[a] for a in range(1, 4)) + even[i][0] * sums[0]
        second = sum(odd[i][a] * gaps[a] for a in range(1, 4)) + odd[i][0] * gaps[0]
        result[i] = first + second
        result[7 - i] = first - second if sign > 0 else second - first
    return result


def quadratic(values):
    sums = [values[a] + values[7 - a] for a in range(4)]
    gaps = [values[a] - values[7 - a] for a in range(4)]
    result = None
    for table, part in zip(SQUARES, (sums, gaps)):
        for r in range(4):
            if table[r][r] == 0.0:
                continue
            term = table[r][r] * part[r]
            for c in range(r + 1, 4):
                term = term + table[r][c] * part[c]
            term = term * term
            result = term if result is None else result + term
    return result


def rows(start):
    return pl.ds(pl.multiple_of(start, 8), 8)


def every_eighth(start):
    return pl.ds(start, 8, stride=8)


def far_first(count):
    return sorted(range(1, count), key=lambda step: (abs(2 * step - count), step))


def sublane_sum(value):
    return jnp.sum(value, axis=0, keepdims=True)


def split(value):
    high = value.astype(jnp.bfloat16)
    low = (value - high.astype(jnp.float32)).astype(jnp.bfloat16)
    return high, low


def dot(first, second, dims):
    return lax.dot_general(
        first, second, (dims, ((), ())), preferred_element_type=jnp.float32
    )


def face_slice(face, base, step):
    direction, level = face // 2, 7 * (face % 2)
    if direction == 0:
        return pl.ds(pl.multiple_of(base + 64 * level + 8 * step, 8), 8)
    if direction == 1:
        return pl.ds(pl.multiple_of(base + 64 * step + 8 * level, 8), 8)
    return pl.ds(base + 64 * step + level, 8, stride=8)


def kernel(
    sizes,
    adjoint_hbm,
    velocity_hbm,
    geometry_hbm,
    codes_hbm,
    first,
    image,
    factor_ref,
    adjoint,
    velocity,
    geometry,
    codes,
    mass,
    along_i,
    along_k,
    columns,
    pairs,
    chosen,
    faces,
    gained,
    outgoing,
    incoming,
    partial,
    near_slots,
    far_slots,
    load_sem,
    face_send,
    face_recv,
    near_send,
    near_recv,
    far_send,
    far_recv,
):
    owners, n_y, n_z = sizes
    n_x = owners // 2
    me = lax.axis_index("sub")
    group = lax.axis_index("grp")
    my_y = group // n_z
    my_z = group - my_y * n_z
    my_x = me // 2
    my_core = me - my_x * 2

    def load(index, source, target):
        return pltpu.make_async_copy(source, target, load_sem.at[index])

    loads = [load(0, codes_hbm, codes), load(1, geometry_hbm, geometry)]
    loads.append(load(2, velocity_hbm, velocity))
    for index, (low, high) in enumerate(GROUPS):
        part = pl.ds(low * POINTS, (high - low) * POINTS)
        loads.append(load(3 + index, adjoint_hbm.at[part], adjoint.at[part]))
    for copy in loads:
        copy.start()

    barrier = pltpu.get_barrier_semaphore()
    n_near, n_far = 2 * n_z, n_x * n_y
    near_me = my_z * 2 + my_core
    far_me = my_y * n_x + my_x

    def sub_peer(step):
        return {"grp": group, "sub": lax.rem(me + step, owners)}

    def near_peer(step):
        place = lax.rem(near_me + step, n_near)
        z = place // 2
        return {"grp": my_y * n_z + z, "sub": my_x * 2 + (place - z * 2)}

    def far_peer(step):
        place = lax.rem(far_me + step, n_far)
        y = place // n_x
        return {"grp": y * n_z + my_z, "sub": (place - y * n_x) * 2 + my_core}

    for count, peer in ((owners, sub_peer), (n_near, near_peer), (n_far, far_peer)):

        def greet(step, carry, peer=peer):
            pl.semaphore_signal(barrier, inc=1, device_id=peer(step), device_id_type=MESH)
            return carry

        lax.fori_loop(1, count, greet, 0, unroll=4)

    sublane = lax.broadcasted_iota(jnp.int32, (8, 128), 0)
    lane = lax.broadcasted_iota(jnp.int32, (8, 128), 1).astype(jnp.float32)
    inside = jnp.where((sublane >= 1) & (sublane <= 6), 1.0, 0.0)
    depth_weight = jnp.zeros((8, 128), jnp.float32)
    for k in range(8):
        depth_weight = jnp.where(sublane == k, WEIGHTS[k], depth_weight)
    zero = jnp.zeros((8, 128), jnp.float32)

    loads[0].wait()
    for tile in range(6):
        width = min(128, 704 - 128 * tile)
        row = codes[:, 128 * tile : 128 * tile + width].astype(jnp.float32)
        columns[128 * tile : 128 * tile + width, :] = jnp.transpose(
            jnp.broadcast_to(row, (128, width))
        )
    lane16 = lax.broadcasted_iota(jnp.int32, (16, 128), 1).astype(jnp.float32)
    for block in range(owners):
        code = columns[2 * LPAIR + 16 * block : 2 * LPAIR + 16 * block + 16, :]
        for face in range(6):
            chosen[16 * block : 16 * block + 16, 128 * face : 128 * face + 128] = jnp.where(
                code == lane16 + float(128 * face), 1.0, 0.0
            ).astype(jnp.bfloat16)
    for turn in range(2):
        own = pl.ds(pl.multiple_of(me * FMAX, FMAX), FMAX)
        for index in range(len(GROUPS)):
            outgoing[turn, index] = jnp.zeros((128, 128), jnp.float32)
            incoming[turn, index, own, :] = jnp.zeros((FMAX, 128), jnp.float32)

    loads[1].wait()
    volume = jnp.broadcast_to(geometry[0:1, :], (8, 128))
    inverse = [jnp.broadcast_to(geometry[d : d + 1, :], (8, 128)) for d in range(1, 4)]
    squared = [value * value for value in inverse]
    weighted = volume * depth_weight
    for i in range(8):
        for j in range(8):
            mass[64 * i + 8 * j : 64 * i + 8 * j + 8, :] = weighted * (WEIGHTS[i] * WEIGHTS[j])
    loads[2].wait()

    def scale_velocity(index, carry):
        for d in range(3):
            place = rows(index * 8 + d * POINTS)
            velocity[place, :] = velocity[place, :] * inverse[d]
        return carry

    lax.fori_loop(0, 64, scale_velocity, 0, unroll=4)

    def build_pairs():
        def find(index, found):
            here = columns[rows(index * 8), :]
            there = columns[rows(index * 8 + LPAIR), :]
            result = []
            for face in range(6):
                place = lane + float(128 * face)
                value = jnp.where(here == place, there, found[face])
                result.append(jnp.where(there == place, here, value))
            return tuple(result)

        found = lax.fori_loop(0, LPAIR // 8, find, (zero - 1.0,) * 6, unroll=4)
        partner = [
            jnp.broadcast_to(jnp.max(value, axis=0, keepdims=True), (16, 128)) for value in found
        ]
        row_id = lax.broadcasted_iota(jnp.int32, (16, 128), 0).astype(jnp.float32)

        def mark(index, carry):
            place = row_id + (index * 16).astype(jnp.float32)
            here = pl.ds(pl.multiple_of(index * 16, 16), 16)
            for face in range(6):
                pairs[here, 128 * face : 128 * face + 128] = jnp.where(
                    partner[face] == place, 1.0, 0.0
                ).astype(jnp.bfloat16)
            return carry

        lax.fori_loop(0, 48, mark, 0, unroll=8)

    def sweep(source, base, table, factors, finish):
        def lines(r, carry):
            values = [source[rows(base + 64 * i + 8 * r), :] for i in range(8)]
            moved = product(values, table)
            for i in range(8):
                along_i[rows(64 * i + 8 * r), :] = (
                    values[i] * (1.0 / TIME_STEP) + factors(0, 64 * i + 8 * r) * moved[i]
                )
            values = [source[every_eighth(base + 64 * r + k), :] for k in range(8)]
            moved = product(values, table)
            for k in range(8):
                along_k[every_eighth(64 * r + k), :] = moved[k]
            return carry

        lax.fori_loop(0, 8, lines, 0, unroll=True)

        def close(i, carry):
            values = [source[rows(base + 64 * i + 8 * j), :] for j in range(8)]
            moved = product(values, table)
            for j in range(8):
                place = 64 * i + 8 * j
                total = along_i[rows(place), :] + factors(1, place) * moved[j]
                total = total + factors(2, place) * along_k[rows(place), :]
                carry = finish(place, values[j], mass[rows(place), :] * total, carry)
            return carry

        return lax.fori_loop(0, 8, close, (zero, zero), unroll=True)

    def note(quantity, comp, value):
        partial[pl.ds(quantity * 8 + comp, 1), :] = sublane_sum(value)

    def force(comp, carry):
        base = pl.multiple_of(comp * POINTS, POINTS)

        def finish(place, value, total, sums):
            first[rows(base + place), :] = total
            return sums[0] + total * total, sums[1]

        sums = sweep(
            adjoint,
            base,
            DERIVATIVE_HALVES,
            lambda d, place: velocity[rows(d * POINTS + place), :],
            finish,
        )
        note(0, comp, sums[0])
        return carry

    def kappas(comp):
        kappa = jnp.where(comp == 3, DIFFUSIVITY[3], DIFFUSIVITY[0])
        kappa = jnp.where(comp == 4, DIFFUSIVITY[4], kappa)
        return [kappa * value for value in squared]

    def spread(comp, carry):
        base = pl.multiple_of(comp * POINTS, POINTS)
        scaled = kappas(comp)

        def finish(place, value, total, sums):
            image[rows(base + place), :] = total
            return sums[0] + value * total, sums[1] + total * total

        sums = sweep(first, base, STIFFNESS_HALVES, lambda d, place: scaled[d], finish)
        note(1, comp, sums[0])
        note(2, comp, sums[1])
        return carry

    def energy(comp, carry):
        base = pl.multiple_of(comp * POINTS, POINTS)
        scaled = kappas(comp)
        forms = [zero, zero, zero]
        plain = zero
        for r in range(8):
            lines_i = [image[rows(base + 64 * i + 8 * r), :] for i in range(8)]
            forms[0] = forms[0] + WEIGHTS[r] * quadratic(lines_i)
            lines_j = [image[rows(base + 64 * r + 8 * j), :] for j in range(8)]
            forms[1] = forms[1] + WEIGHTS[r] * quadratic(lines_j)
            lines_k = [image[every_eighth(base + 64 * r + k), :] for k in range(8)]
            forms[2] = forms[2] + WEIGHTS[r] * quadratic(lines_k)
            level = [lines_j[j] * lines_j[j] for j in range(8)]
            level = sum((WEIGHTS[j] * (level[j] + level[7 - j]) for j in range(1, 4)), WEIGHTS[0] * (level[0] + level[7]))
            plain = plain + WEIGHTS[r] * level
        total = plain * (1.0 / TIME_STEP)
        for d in range(3):
            total = total + scaled[d] * forms[d]
        note(3, comp, weighted * total)
        return carry

    def face_copy(turn, index, step):
        peer = sub_peer(step)
        return pltpu.make_async_remote_copy(
            src_ref=outgoing.at[turn, index, pl.ds(pl.multiple_of(peer["sub"] * FMAX, FMAX), FMAX)],
            dst_ref=incoming.at[turn, index, pl.ds(pl.multiple_of(me * FMAX, FMAX), FMAX)],
            send_sem=face_send.at[turn, index, step],
            recv_sem=face_recv.at[turn, index, step],
            device_id=peer,
            device_id_type=MESH,
        )

    def each_copy(turn, index, act):
        for step in far_first(owners):
            act(face_copy(turn, index, step))

    def send(turn, index, field):
        low, high = GROUPS[index]

        def gather(comp, carry):
            base = pl.multiple_of(comp * POINTS, POINTS)
            top = pl.multiple_of(comp * FACE_ROWS, 16)
            for face in range(6):
                block = jnp.concatenate(
                    [field[face_slice(face, base, a), :] * inside for a in range(1, 7)], axis=0
                )
                big, small = split(block)
                place = slice(128 * face, 128 * face + 128)
                faces[pl.ds(top, FACE_ROWS), place] = big
                faces[pl.ds(pl.multiple_of(top + HALF_ROWS, 16), FACE_ROWS), place] = small
            return carry

        lax.fori_loop(low, high, gather, 0, unroll=True)
        start, stop = low * FACE_ROWS, high * FACE_ROWS
        over_lanes = ((1,), (1,))
        outgoing[turn, index, :, 0 : stop - start] = dot(
            chosen[...], faces[start:stop, :], over_lanes
        ) + dot(chosen[...], faces[HALF_ROWS + start : HALF_ROWS + stop, :], over_lanes)
        if turn == 0 and index == 0:
            pl.semaphore_wait(barrier, owners - 1 + n_near - 1 + n_far - 1)
        each_copy(turn, index, lambda copy: copy.start())

    plain_dims = ((1,), (0,))

    def local():
        for part in range(3):
            place = slice(256 * part, 256 * part + 256)
            gained[:, place] = dot(faces[0:HALF_ROWS, :], pairs[:, place], plain_dims) + dot(
                faces[HALF_ROWS:, :], pairs[:, place], plain_dims
            )

    def receive(turn, index, field, quantity):
        low, high = GROUPS[index]
        start, stop = low * FACE_ROWS, high * FACE_ROWS
        each_copy(turn, index, lambda copy: copy.wait_recv())
        big, small = split(jnp.transpose(incoming[turn, index])[0 : stop - start, :])
        for part in range(3):
            place = slice(256 * part, 256 * part + 256)
            gained[start:stop, place] = (
                gained[start:stop, place]
                + dot(big, chosen[:, place], plain_dims)
                + dot(small, chosen[:, place], plain_dims)
            )

        def add(comp, carry):
            base = pl.multiple_of(comp * POINTS, POINTS)
            places = [face_slice(face, base, a + 1) for face in range(6) for a in range(6)]
            values = [field[place, :] for place in places]
            extra = [
                gained[rows(comp * FACE_ROWS + 8 * a), 128 * face : 128 * face + 128]
                for face in range(6)
                for a in range(6)
            ]
            sums = zero
            for place, value, more in zip(places, values, extra):
                sums = sums + value * more
                field[place, :] = value + more
            here = pl.ds(quantity * 8 + comp, 1)
            partial[here, :] = partial[here, :] + sublane_sum(sums)
            return carry

        lax.fori_loop(low, high, add, 0, unroll=True)

    faces[COMP * FACE_ROWS : HALF_ROWS, :] = jnp.zeros((16, 768), jnp.bfloat16)
    faces[HALF_ROWS + COMP * FACE_ROWS :, :] = jnp.zeros((16, 768), jnp.bfloat16)
    partial[...] = jnp.zeros((32, 128), jnp.float32)

    for index, (low, high) in enumerate(GROUPS):
        loads[3 + index].wait()
        lax.fori_loop(low, high, force, 0, unroll=True)
        send(0, index, first)
    build_pairs()
    local()
    for index, (low, high) in enumerate(GROUPS):
        receive(0, index, first, 0)
        lax.fori_loop(low, high, spread, 0, unroll=True)
        send(1, index, image)
    local()
    for index, (low, high) in enumerate(GROUPS):
        receive(1, index, image, 2)
        lax.fori_loop(low, high, energy, 0, unroll=True)

    entry = lax.broadcasted_iota(jnp.int32, (32, 128), 0)
    column = lax.broadcasted_iota(jnp.int32, (32, 128), 1)
    diagonal = entry == column
    whole = jnp.sum(partial[...], axis=1, keepdims=True)
    row = jnp.sum(jnp.where(diagonal, whole, 0.0), axis=0, keepdims=True)

    def sum_copy(slots, mine, peer, send_sems, recv_sems, step):
        return pltpu.make_async_remote_copy(
            src_ref=slots.at[mine],
            dst_ref=slots.at[mine],
            send_sem=send_sems.at[step],
            recv_sem=recv_sems.at[step],
            device_id=peer(step),
            device_id_type=MESH,
        )

    stages = (
        (near_slots, n_near, near_me, near_peer, near_send, near_recv),
        (far_slots, n_far, far_me, far_peer, far_send, far_recv),
    )
    for slots, count, mine, peer, send_sems, recv_sems in stages:
        slots[mine] = row

        for step in far_first(count):
            sum_copy(slots, mine, peer, send_sems, recv_sems, step).start()
        for step in range(1, count):
            sum_copy(slots, mine, peer, send_sems, recv_sems, step).wait_recv()
        row = jnp.sum(slots[...], axis=0)

    spreaded = jnp.where(diagonal, jnp.broadcast_to(row, (32, 128)), 0.0)
    totals = jnp.broadcast_to(jnp.sum(spreaded, axis=1, keepdims=True), (32, 128))
    bb, bq, qq, qhq = (totals[8 * n : 8 * n + 8] for n in range(4))
    alpha = bb / bq
    scaled_qq = alpha * qq
    norm_next = alpha * scaled_qq - bb
    beta = norm_next / bb
    up = 1.0 + beta
    curve = up * (up * bq - 2.0 * scaled_qq) + alpha * (alpha * qhq)
    alpha_next = norm_next / curve
    factor_ref[0:8, :] = alpha + alpha_next * up
    factor_ref[8:16, :] = -alpha * alpha_next

    for turn in range(2):
        for index in range(len(GROUPS)):
            each_copy(turn, index, lambda copy: copy.wait_send())
    for slots, count, mine, peer, send_sems, recv_sems in stages:

        for step in range(1, count):
            sum_copy(slots, mine, peer, send_sems, recv_sems, step).wait_send()


def solution(mesh):
    owners, groups = mesh.shape["sub"], mesh.shape["grp"]
    n_z = 12 if groups % 12 == 0 else max(1, groups // 2)
    n_y = groups // n_z

    def shards(adjoint, velocity, geometry, face_codes):
        elements = adjoint.shape[2]
        flat = COMP * POINTS
        vmem = pltpu.VMEM
        f32, bf16 = jnp.float32, jnp.bfloat16
        hbm = pl.BlockSpec(memory_space=pltpu.HBM)

        def keep(array):
            return pltpu.with_memory_space_constraint(array, pltpu.HBM)

        inner = pl.BlockSpec(memory_space=pltpu.VMEM)
        n_near, n_far = 2 * n_z, n_y * owners // 2
        dma = pltpu.SemaphoreType.DMA
        first, image, factor = pl.pallas_call(
            functools.partial(kernel, (owners, n_y, n_z)),
            out_shape=(
                pltpu.VMEM((flat, elements), f32),
                pltpu.VMEM((flat, elements), f32),
                pltpu.VMEM((16, elements), f32),
            ),
            in_specs=[hbm] * 4,
            out_specs=(inner, inner, inner),
            scratch_shapes=[
                vmem((flat, elements), f32),
                vmem((3 * POINTS, elements), f32),
                vmem((4, elements), f32),
                vmem((1, 704), jnp.int32),
                vmem((POINTS, elements), f32),
                vmem((POINTS, elements), f32),
                vmem((POINTS, elements), f32),
                vmem((704, 128), f32),
                vmem((768, 768), bf16),
                vmem((128, 768), bf16),
                vmem((2 * HALF_ROWS, 768), bf16),
                vmem((HALF_ROWS, 768), f32),
                vmem((2, len(GROUPS), 128, 128), f32),
                vmem((2, len(GROUPS), 128, 128), f32),
                vmem((32, 128), f32),
                vmem((n_near, 1, 128), f32),
                vmem((n_far, 1, 128), f32),
                dma((3 + len(GROUPS),)),
                dma((2, len(GROUPS), owners)),
                dma((2, len(GROUPS), owners)),
                dma((n_near,)),
                dma((n_near,)),
                dma((n_far,)),
                dma((n_far,)),
            ],
            compiler_params=pltpu.CompilerParams(
                collective_id=0, has_side_effects=True, vmem_limit_bytes=32 * 1024 * 1024
            ),
        )(
            keep(adjoint.reshape(flat, elements)),
            keep(velocity.reshape(3 * POINTS, elements)),
            keep(geometry),
            keep(face_codes),
        )
        shape = (COMP, POINTS, elements)
        return (
            factor[0:COMP, None, :] * first.reshape(shape)
            + factor[8 : 8 + COMP, None, :] * image.reshape(shape)
        )

    placed = (
        P(None, None, ("grp", "sub")),
        P(None, None, ("grp", "sub")),
        P(None, ("grp", "sub")),
        P(("grp", "sub"), None),
    )
    return jax.shard_map(
        shards, mesh=mesh, in_specs=placed, out_specs=P(None, None, ("grp", "sub")), check_vma=False
    )
```

```python
import functools

import jax
import jax.numpy as jnp
from jax import lax
from jax.experimental import pallas as pl
from jax.experimental.pallas import tpu as pltpu
from jax.sharding import PartitionSpec as P

MESH = pl.DeviceIdType.MESH
COMP = 5
POINTS = 512
LPAIR = 288
FMAX = 16
FACE_ROWS = 48
HALF_ROWS = 256
TIME_STEP = 0.05
DIFFUSIVITY = (1.0, 1.0, 1.0, 0.7, 0.2)
GLL_POINTS = (
    -1.0,
    -0.8717401485096066,
    -0.5917001814331423,
    -0.2092992179024789,
    0.2092992179024789,
    0.5917001814331423,
    0.8717401485096066,
    1.0,
)


def legendre_seven(point):
    before = 1.0
    current = point
    for order in range(1, 7):
        following = ((2 * order + 1) * point * current - order * before) / (order + 1)
        before = current
        current = following
    return current


def gll_tables():
    points = list(GLL_POINTS)
    values = [legendre_seven(point) for point in points]
    weights = [2.0 / (56.0 * value * value) for value in values]
    derivative = []
    for row in range(8):
        line = []
        for col in range(8):
            if row == col:
                line.append(0.0)
            else:
                line.append(values[row] / (values[col] * (points[row] - points[col])))
        derivative.append(line)
    derivative[0][0] = -14.0
    derivative[7][7] = 14.0
    stiffness = []
    for row in range(8):
        line = []
        for col in range(8):
            total = 0.0
            for mid in range(8):
                total += derivative[mid][row] * weights[mid] * derivative[mid][col]
            line.append(total / weights[row])
        stiffness.append(line)
    return weights, derivative, stiffness


def halves(matrix):
    even = [[0.5 * (matrix[i][a] + matrix[i][7 - a]) for a in range(4)] for i in range(4)]
    odd = [[0.5 * (matrix[i][a] - matrix[i][7 - a]) for a in range(4)] for i in range(4)]
    return even, odd


def triangle(matrix):
    result = [[0.0] * 4 for _ in range(4)]
    for r in range(4):
        pivot = matrix[r][r] - sum(result[m][r] ** 2 for m in range(r))
        if pivot < 1e-9 * matrix[r][r]:
            continue
        result[r][r] = pivot**0.5
        for c in range(r + 1, 4):
            rest = matrix[r][c] - sum(result[m][r] * result[m][c] for m in range(r))
            result[r][c] = rest / result[r][r]
    return result


WEIGHTS, DERIVATIVE, STIFFNESS = gll_tables()
SYMMETRIC_HALVES = halves([[WEIGHTS[i] * v for v in STIFFNESS[i]] for i in range(8)])
SQUARES = tuple(triangle(part) for part in SYMMETRIC_HALVES)
GROUPS = ((0, 2), (2, 4), (4, 5))
DERIVATIVE_HALVES = halves(DERIVATIVE) + (-1,)
STIFFNESS_HALVES = halves(STIFFNESS) + (1,)


def product(values, table):
    even, odd, sign = table
    sums = [values[a] + values[7 - a] for a in range(4)]
    gaps = [values[a] - values[7 - a] for a in range(4)]
    steps = [sums[a] - sums[3] for a in range(3)]
    result = [None] * 8
    for i in range(4):
        first = even[i][0] * steps[0] + even[i][1] * steps[1] + even[i][2] * steps[2]
        second = sum(odd[i][a] * gaps[a] for a in range(1, 4)) + odd[i][0] * gaps[0]
        result[i] = first + second
        result[7 - i] = first - second if sign > 0 else second - first
    return result


def quadratic(values):
    sums = [values[a] + values[7 - a] for a in range(4)]
    gaps = [values[a] - values[7 - a] for a in range(4)]
    result = None
    for table, part in zip(SQUARES, (sums, gaps)):
        for r in range(4):
            if table[r][r] == 0.0:
                continue
            term = table[r][r] * part[r]
            for c in range(r + 1, 4):
                term = term + table[r][c] * part[c]
            term = term * term
            result = term if result is None else result + term
    return result


def rows(start):
    return pl.ds(pl.multiple_of(start, 8), 8)


def every_eighth(start):
    return pl.ds(start, 8, stride=8)


def far_first(count):
    return sorted(range(1, count), key=lambda step: (abs(2 * step - count), step))


def sublane_sum(value):
    return jnp.sum(value, axis=0, keepdims=True)


def split(value):
    high = value.astype(jnp.bfloat16)
    low = (value - high.astype(jnp.float32)).astype(jnp.bfloat16)
    return high, low


def dot(first, second, dims):
    return lax.dot_general(
        first, second, (dims, ((), ())), preferred_element_type=jnp.float32
    )


def face_slice(face, base, step):
    direction, level = face // 2, 7 * (face % 2)
    if direction == 0:
        return pl.ds(pl.multiple_of(base + 64 * level + 8 * step, 8), 8)
    if direction == 1:
        return pl.ds(pl.multiple_of(base + 64 * step + 8 * level, 8), 8)
    return pl.ds(base + 64 * step + level, 8, stride=8)


def kernel(
    sizes,
    adjoint_hbm,
    velocity_hbm,
    geometry_hbm,
    codes_hbm,
    first,
    image,
    factor_ref,
    adjoint,
    velocity,
    geometry,
    codes,
    mass,
    along_i,
    along_k,
    columns,
    pairs,
    chosen,
    faces,
    gained,
    outgoing,
    incoming,
    partial,
    near_slots,
    far_slots,
    load_sem,
    face_send,
    face_recv,
    near_send,
    near_recv,
    far_send,
    far_recv,
):
    owners, n_y, n_z = sizes
    n_x = owners // 2
    me = lax.axis_index("sub")
    group = lax.axis_index("grp")
    my_y = group // n_z
    my_z = group - my_y * n_z
    my_x = me // 2
    my_core = me - my_x * 2

    def load(index, source, target):
        return pltpu.make_async_copy(source, target, load_sem.at[index])

    loads = [load(0, codes_hbm, codes), load(1, geometry_hbm, geometry)]
    loads.append(load(2, velocity_hbm, velocity))
    for index, (low, high) in enumerate(GROUPS):
        part = pl.ds(low * POINTS, (high - low) * POINTS)
        loads.append(load(3 + index, adjoint_hbm.at[part], adjoint.at[part]))
    for copy in loads:
        copy.start()

    barrier = pltpu.get_barrier_semaphore()
    n_near, n_far = 2 * n_z, n_x * n_y
    near_me = my_z * 2 + my_core
    far_me = my_y * n_x + my_x

    def sub_peer(step):
        return {"grp": group, "sub": lax.rem(me + step, owners)}

    def near_peer(step):
        place = lax.rem(near_me + step, n_near)
        z = place // 2
        return {"grp": my_y * n_z + z, "sub": my_x * 2 + (place - z * 2)}

    def far_peer(step):
        place = lax.rem(far_me + step, n_far)
        y = place // n_x
        return {"grp": y * n_z + my_z, "sub": (place - y * n_x) * 2 + my_core}

    for count, peer in ((owners, sub_peer), (n_near, near_peer), (n_far, far_peer)):

        def greet(step, carry, peer=peer):
            pl.semaphore_signal(barrier, inc=1, device_id=peer(step), device_id_type=MESH)
            return carry

        lax.fori_loop(1, count, greet, 0, unroll=4)

    sublane = lax.broadcasted_iota(jnp.int32, (8, 128), 0)
    lane = lax.broadcasted_iota(jnp.int32, (8, 128), 1).astype(jnp.float32)
    inside = jnp.where((sublane >= 1) & (sublane <= 6), 1.0, 0.0)
    depth_weight = jnp.zeros((8, 128), jnp.float32)
    for k in range(8):
        depth_weight = jnp.where(sublane == k, WEIGHTS[k], depth_weight)
    zero = jnp.zeros((8, 128), jnp.float32)

    loads[0].wait()
    for tile in range(6):
        width = min(128, 704 - 128 * tile)
        row = codes[:, 128 * tile : 128 * tile + width].astype(jnp.float32)
        columns[128 * tile : 128 * tile + width, :] = jnp.transpose(
            jnp.broadcast_to(row, (128, width))
        )
    lane16 = lax.broadcasted_iota(jnp.int32, (16, 128), 1).astype(jnp.float32)
    for block in range(owners):
        code = columns[2 * LPAIR + 16 * block : 2 * LPAIR + 16 * block + 16, :]
        for face in range(6):
            chosen[16 * block : 16 * block + 16, 128 * face : 128 * face + 128] = jnp.where(
                code == lane16 + float(128 * face), 1.0, 0.0
            ).astype(jnp.bfloat16)
    for turn in range(2):
        own = pl.ds(pl.multiple_of(me * FMAX, FMAX), FMAX)
        for index in range(len(GROUPS)):
            outgoing[turn, index] = jnp.zeros((128, 128), jnp.float32)
            incoming[turn, index, own, :] = jnp.zeros((FMAX, 128), jnp.float32)

    loads[1].wait()
    volume = jnp.broadcast_to(geometry[0:1, :], (8, 128))
    inverse = [jnp.broadcast_to(geometry[d : d + 1, :], (8, 128)) for d in range(1, 4)]
    squared = [value * value for value in inverse]
    weighted = volume * depth_weight
    for i in range(8):
        for j in range(8):
            mass[64 * i + 8 * j : 64 * i + 8 * j + 8, :] = weighted * (WEIGHTS[i] * WEIGHTS[j])
    loads[2].wait()

    def scale_velocity(index, carry):
        for d in range(3):
            place = rows(index * 8 + d * POINTS)
            velocity[place, :] = velocity[place, :] * inverse[d]
        return carry

    lax.fori_loop(0, 64, scale_velocity, 0, unroll=4)

    def build_pairs():
        def find(index, found):
            here = columns[rows(index * 8), :]
            there = columns[rows(index * 8 + LPAIR), :]
            result = []
            for face in range(6):
                place = lane + float(128 * face)
                value = jnp.where(here == place, there, found[face])
                result.append(jnp.where(there == place, here, value))
            return tuple(result)

        found = lax.fori_loop(0, LPAIR // 8, find, (zero - 1.0,) * 6, unroll=4)
        partner = [
            jnp.broadcast_to(jnp.max(value, axis=0, keepdims=True), (16, 128)) for value in found
        ]
        row_id = lax.broadcasted_iota(jnp.int32, (16, 128), 0).astype(jnp.float32)

        def mark(index, carry):
            place = row_id + (index * 16).astype(jnp.float32)
            here = pl.ds(pl.multiple_of(index * 16, 16), 16)
            for face in range(6):
                pairs[here, 128 * face : 128 * face + 128] = jnp.where(
                    partner[face] == place, 1.0, 0.0
                ).astype(jnp.bfloat16)
            return carry

        lax.fori_loop(0, 48, mark, 0, unroll=8)

    def sweep(source, base, table, factors, finish):
        def lines(r, carry):
            values = [source[rows(base + 64 * i + 8 * r), :] for i in range(8)]
            moved = product(values, table)
            for i in range(8):
                along_i[rows(64 * i + 8 * r), :] = (
                    values[i] * (1.0 / TIME_STEP) + factors(0, 64 * i + 8 * r) * moved[i]
                )
            values = [source[every_eighth(base + 64 * r + k), :] for k in range(8)]
            moved = product(values, table)
            for k in range(8):
                along_k[every_eighth(64 * r + k), :] = moved[k]
            return carry

        lax.fori_loop(0, 8, lines, 0, unroll=True)

        def close(i, carry):
            values = [source[rows(base + 64 * i + 8 * j), :] for j in range(8)]
            moved = product(values, table)
            for j in range(8):
                place = 64 * i + 8 * j
                total = along_i[rows(place), :] + factors(1, place) * moved[j]
                total = total + factors(2, place) * along_k[rows(place), :]
                carry = finish(place, values[j], mass[rows(place), :] * total, carry)
            return carry

        return lax.fori_loop(0, 8, close, (zero, zero), unroll=True)

    def note(quantity, comp, value):
        partial[pl.ds(quantity * 8 + comp, 1), :] = sublane_sum(value)

    def force(comp, carry):
        base = pl.multiple_of(comp * POINTS, POINTS)

        def finish(place, value, total, sums):
            first[rows(base + place), :] = total
            return sums[0] + total * total, sums[1]

        sums = sweep(
            adjoint,
            base,
            DERIVATIVE_HALVES,
            lambda d, place: velocity[rows(d * POINTS + place), :],
            finish,
        )
        note(0, comp, sums[0])
        return carry

    def kappas(comp):
        kappa = jnp.where(comp == 3, DIFFUSIVITY[3], DIFFUSIVITY[0])
        kappa = jnp.where(comp == 4, DIFFUSIVITY[4], kappa)
        return [kappa * value for value in squared]

    def spread(comp, carry):
        base = pl.multiple_of(comp * POINTS, POINTS)
        scaled = kappas(comp)

        def finish(place, value, total, sums):
            image[rows(base + place), :] = total
            return sums[0] + value * total, sums[1] + total * total

        sums = sweep(first, base, STIFFNESS_HALVES, lambda d, place: scaled[d], finish)
        note(1, comp, sums[0])
        note(2, comp, sums[1])
        return carry

    def energy(comp, carry):
        base = pl.multiple_of(comp * POINTS, POINTS)
        scaled = kappas(comp)
        forms = [zero, zero, zero]
        plain = zero
        for r in range(8):
            lines_i = [image[rows(base + 64 * i + 8 * r), :] for i in range(8)]
            forms[0] = forms[0] + WEIGHTS[r] * quadratic(lines_i)
            lines_j = [image[rows(base + 64 * r + 8 * j), :] for j in range(8)]
            forms[1] = forms[1] + WEIGHTS[r] * quadratic(lines_j)
            lines_k = [image[every_eighth(base + 64 * r + k), :] for k in range(8)]
            forms[2] = forms[2] + WEIGHTS[r] * quadratic(lines_k)
            level = [lines_j[j] * lines_j[j] for j in range(8)]
            level = sum((WEIGHTS[j] * (level[j] + level[7 - j]) for j in range(1, 4)), WEIGHTS[0] * (level[0] + level[7]))
            plain = plain + WEIGHTS[r] * level
        total = plain * (1.0 / TIME_STEP)
        for d in range(3):
            total = total + scaled[d] * forms[d]
        note(3, comp, weighted * total)
        return carry

    def face_copy(turn, index, step):
        peer = sub_peer(step)
        return pltpu.make_async_remote_copy(
            src_ref=outgoing.at[turn, index, pl.ds(pl.multiple_of(peer["sub"] * FMAX, FMAX), FMAX)],
            dst_ref=incoming.at[turn, index, pl.ds(pl.multiple_of(me * FMAX, FMAX), FMAX)],
            send_sem=face_send.at[turn, index, step],
            recv_sem=face_recv.at[turn, index, step],
            device_id=peer,
            device_id_type=MESH,
        )

    def each_copy(turn, index, act):
        for step in far_first(owners):
            act(face_copy(turn, index, step))

    def select(turn, index, field):
        low, high = GROUPS[index]

        def gather(comp, carry):
            base = pl.multiple_of(comp * POINTS, POINTS)
            top = pl.multiple_of(comp * FACE_ROWS, 16)
            for face in range(6):
                block = jnp.concatenate(
                    [field[face_slice(face, base, a), :] * inside for a in range(1, 7)], axis=0
                )
                big, small = split(block)
                place = slice(128 * face, 128 * face + 128)
                faces[pl.ds(top, FACE_ROWS), place] = big
                faces[pl.ds(pl.multiple_of(top + HALF_ROWS, 16), FACE_ROWS), place] = small
            return carry

        lax.fori_loop(low, high, gather, 0, unroll=True)
        start, stop = low * FACE_ROWS, high * FACE_ROWS
        over_lanes = ((1,), (1,))
        outgoing[turn, index, :, 0 : stop - start] = dot(
            chosen[...], faces[start:stop, :], over_lanes
        ) + dot(chosen[...], faces[HALF_ROWS + start : HALF_ROWS + stop, :], over_lanes)

    def start(turn, index):
        each_copy(turn, index, lambda copy: copy.start())

    plain_dims = ((1,), (0,))

    def local():
        for part in range(3):
            place = slice(256 * part, 256 * part + 256)
            gained[:, place] = dot(faces[0:HALF_ROWS, :], pairs[:, place], plain_dims) + dot(
                faces[HALF_ROWS:, :], pairs[:, place], plain_dims
            )

    def wait(turn, index):
        each_copy(turn, index, lambda copy: copy.wait_recv())

    def receive(turn, index, field, quantity):
        low, high = GROUPS[index]
        begin, stop = low * FACE_ROWS, high * FACE_ROWS
        big, small = split(jnp.transpose(incoming[turn, index])[0 : stop - begin, :])
        for part in range(3):
            place = slice(256 * part, 256 * part + 256)
            gained[begin:stop, place] = (
                gained[begin:stop, place]
                + dot(big, chosen[:, place], plain_dims)
                + dot(small, chosen[:, place], plain_dims)
            )

        def add(comp, carry):
            base = pl.multiple_of(comp * POINTS, POINTS)
            places = [face_slice(face, base, a + 1) for face in range(6) for a in range(6)]
            values = [field[place, :] for place in places]
            extra = [
                gained[rows(comp * FACE_ROWS + 8 * a), 128 * face : 128 * face + 128]
                for face in range(6)
                for a in range(6)
            ]
            sums = zero
            for place, value, more in zip(places, values, extra):
                sums = sums + value * more
                field[place, :] = value + more
            here = pl.ds(quantity * 8 + comp, 1)
            partial[here, :] = partial[here, :] + sublane_sum(sums)
            return carry

        lax.fori_loop(low, high, add, 0, unroll=True)

    faces[COMP * FACE_ROWS : HALF_ROWS, :] = jnp.zeros((16, 768), jnp.bfloat16)
    faces[HALF_ROWS + COMP * FACE_ROWS :, :] = jnp.zeros((16, 768), jnp.bfloat16)
    partial[...] = jnp.zeros((32, 128), jnp.float32)

    for index, (low, high) in enumerate(GROUPS):
        loads[3 + index].wait()
        lax.fori_loop(low, high, force, 0, unroll=True)
        select(0, index, first)
        if index == 0:
            pl.semaphore_wait(barrier, owners - 1 + n_near - 1 + n_far - 1)
        start(0, index)
    build_pairs()
    local()
    last = len(GROUPS) - 1
    for index, (low, high) in enumerate(GROUPS):
        wait(0, index)
        if index > 0:
            select(1, index - 1, image)
        receive(0, index, first, 0)
        if index > 0:
            start(1, index - 1)
        lax.fori_loop(low, high, spread, 0, unroll=True)
    select(1, last, image)
    start(1, last)
    local()
    for index, (low, high) in enumerate(GROUPS):
        wait(1, index)
        receive(1, index, image, 2)
        lax.fori_loop(low, high, energy, 0, unroll=True)

    entry = lax.broadcasted_iota(jnp.int32, (32, 128), 0)
    column = lax.broadcasted_iota(jnp.int32, (32, 128), 1)
    diagonal = entry == column
    whole = jnp.sum(partial[...], axis=1, keepdims=True)
    row = jnp.sum(jnp.where(diagonal, whole, 0.0), axis=0, keepdims=True)

    def sum_copy(slots, mine, peer, send_sems, recv_sems, step):
        return pltpu.make_async_remote_copy(
            src_ref=slots.at[mine],
            dst_ref=slots.at[mine],
            send_sem=send_sems.at[step],
            recv_sem=recv_sems.at[step],
            device_id=peer(step),
            device_id_type=MESH,
        )

    stages = (
        (near_slots, n_near, near_me, near_peer, near_send, near_recv),
        (far_slots, n_far, far_me, far_peer, far_send, far_recv),
    )
    for slots, count, mine, peer, send_sems, recv_sems in stages:
        slots[mine] = row

        for step in far_first(count):
            sum_copy(slots, mine, peer, send_sems, recv_sems, step).start()
        if slots is near_slots:
            for turn in range(2):
                for index in range(len(GROUPS)):
                    each_copy(turn, index, lambda copy: copy.wait_send())
        for step in far_first(count):
            sum_copy(slots, mine, peer, send_sems, recv_sems, step).wait_send()
        for step in reversed(far_first(count)):
            sum_copy(slots, mine, peer, send_sems, recv_sems, step).wait_recv()
        row = jnp.sum(slots[...], axis=0)

    spreaded = jnp.where(diagonal, jnp.broadcast_to(row, (32, 128)), 0.0)
    totals = jnp.broadcast_to(jnp.sum(spreaded, axis=1, keepdims=True), (32, 128))
    bb, bq, qq, qhq = (totals[8 * n : 8 * n + 8] for n in range(4))
    alpha = bb / bq
    scaled_qq = alpha * qq
    norm_next = alpha * scaled_qq - bb
    beta = norm_next / bb
    up = 1.0 + beta
    curve = up * (up * bq - 2.0 * scaled_qq) + alpha * (alpha * qhq)
    alpha_next = norm_next / curve
    factor_ref[0:8, :] = alpha + alpha_next * up
    factor_ref[8:16, :] = -alpha * alpha_next


def solution(mesh):
    owners, groups = mesh.shape["sub"], mesh.shape["grp"]
    n_z = 12 if groups % 12 == 0 else max(1, groups // 2)
    n_y = groups // n_z

    def shards(adjoint, velocity, geometry, face_codes):
        elements = adjoint.shape[2]
        flat = COMP * POINTS
        vmem = pltpu.VMEM
        f32, bf16 = jnp.float32, jnp.bfloat16
        hbm = pl.BlockSpec(memory_space=pltpu.HBM)

        def keep(array):
            return pltpu.with_memory_space_constraint(array, pltpu.HBM)

        inner = pl.BlockSpec(memory_space=pltpu.VMEM)
        n_near, n_far = 2 * n_z, n_y * owners // 2
        dma = pltpu.SemaphoreType.DMA
        first, image, factor = pl.pallas_call(
            functools.partial(kernel, (owners, n_y, n_z)),
            out_shape=(
                pltpu.VMEM((flat, elements), f32),
                pltpu.VMEM((flat, elements), f32),
                pltpu.VMEM((16, elements), f32),
            ),
            in_specs=[hbm] * 4,
            out_specs=(inner, inner, inner),
            scratch_shapes=[
                vmem((flat, elements), f32),
                vmem((3 * POINTS, elements), f32),
                vmem((4, elements), f32),
                vmem((1, 704), jnp.int32),
                vmem((POINTS, elements), f32),
                vmem((POINTS, elements), f32),
                vmem((POINTS, elements), f32),
                vmem((704, 128), f32),
                vmem((768, 768), bf16),
                vmem((128, 768), bf16),
                vmem((2 * HALF_ROWS, 768), bf16),
                vmem((HALF_ROWS, 768), f32),
                vmem((2, len(GROUPS), 128, 128), f32),
                vmem((2, len(GROUPS), 128, 128), f32),
                vmem((32, 128), f32),
                vmem((n_near, 1, 128), f32),
                vmem((n_far, 1, 128), f32),
                dma((3 + len(GROUPS),)),
                dma((2, len(GROUPS), owners)),
                dma((2, len(GROUPS), owners)),
                dma((n_near,)),
                dma((n_near,)),
                dma((n_far,)),
                dma((n_far,)),
            ],
            compiler_params=pltpu.CompilerParams(
                collective_id=0, has_side_effects=True, vmem_limit_bytes=32 * 1024 * 1024
            ),
        )(
            keep(adjoint.reshape(flat, elements)),
            keep(velocity.reshape(3 * POINTS, elements)),
            keep(geometry),
            keep(face_codes),
        )
        shape = (COMP, POINTS, elements)
        return (
            factor[0:COMP, None, :] * first.reshape(shape)
            + factor[8 : 8 + COMP, None, :] * image.reshape(shape)
        )

    placed = (
        P(None, None, ("grp", "sub")),
        P(None, None, ("grp", "sub")),
        P(None, ("grp", "sub")),
        P(("grp", "sub"), None),
    )
    return jax.shard_map(
        shards, mesh=mesh, in_specs=placed, out_specs=P(None, None, ("grp", "sub")), check_vma=False
    )
```

```python
import functools

import jax
import jax.numpy as jnp
from jax import lax
from jax.experimental import pallas as pl
from jax.experimental.pallas import tpu as pltpu
from jax.sharding import PartitionSpec as P

MESH = pl.DeviceIdType.MESH
COMP = 5
POINTS = 512
LPAIR = 288
FMAX = 16
FACE_ROWS = 48
HALF_ROWS = 256
TIME_STEP = 0.05
DIFFUSIVITY = (1.0, 1.0, 1.0, 0.7, 0.2)
GLL_POINTS = (
    -1.0,
    -0.8717401485096066,
    -0.5917001814331423,
    -0.2092992179024789,
    0.2092992179024789,
    0.5917001814331423,
    0.8717401485096066,
    1.0,
)


def legendre_seven(point):
    before = 1.0
    current = point
    for order in range(1, 7):
        following = ((2 * order + 1) * point * current - order * before) / (order + 1)
        before = current
        current = following
    return current


def gll_tables():
    points = list(GLL_POINTS)
    values = [legendre_seven(point) for point in points]
    weights = [2.0 / (56.0 * value * value) for value in values]
    derivative = []
    for row in range(8):
        line = []
        for col in range(8):
            if row == col:
                line.append(0.0)
            else:
                line.append(values[row] / (values[col] * (points[row] - points[col])))
        derivative.append(line)
    derivative[0][0] = -14.0
    derivative[7][7] = 14.0
    stiffness = []
    for row in range(8):
        line = []
        for col in range(8):
            total = 0.0
            for mid in range(8):
                total += derivative[mid][row] * weights[mid] * derivative[mid][col]
            line.append(total / weights[row])
        stiffness.append(line)
    return weights, derivative, stiffness


def halves(matrix):
    even = [[0.5 * (matrix[i][a] + matrix[i][7 - a]) for a in range(4)] for i in range(4)]
    odd = [[0.5 * (matrix[i][a] - matrix[i][7 - a]) for a in range(4)] for i in range(4)]
    return even, odd


def triangle(matrix):
    result = [[0.0] * 4 for _ in range(4)]
    for r in range(4):
        pivot = matrix[r][r] - sum(result[m][r] ** 2 for m in range(r))
        if pivot < 1e-9 * matrix[r][r]:
            continue
        result[r][r] = pivot**0.5
        for c in range(r + 1, 4):
            rest = matrix[r][c] - sum(result[m][r] * result[m][c] for m in range(r))
            result[r][c] = rest / result[r][r]
    return result


WEIGHTS, DERIVATIVE, STIFFNESS = gll_tables()
SYMMETRIC_HALVES = halves([[WEIGHTS[i] * v for v in STIFFNESS[i]] for i in range(8)])
SQUARES = tuple(triangle(part) for part in SYMMETRIC_HALVES)
GROUPS = ((0, 2), (2, 4), (4, 5))
DERIVATIVE_HALVES = halves(DERIVATIVE) + (-1,)
STIFFNESS_HALVES = halves(STIFFNESS) + (1,)


def product(values, table):
    even, odd, sign = table
    sums = [values[a] + values[7 - a] for a in range(4)]
    gaps = [values[a] - values[7 - a] for a in range(4)]
    steps = [sums[a] - sums[3] for a in range(3)]
    result = [None] * 8
    for i in range(4):
        first = even[i][0] * steps[0] + even[i][1] * steps[1] + even[i][2] * steps[2]
        second = sum(odd[i][a] * gaps[a] for a in range(1, 4)) + odd[i][0] * gaps[0]
        result[i] = first + second
        result[7 - i] = first - second if sign > 0 else second - first
    return result


def quadratic(values):
    sums = [values[a] + values[7 - a] for a in range(4)]
    gaps = [values[a] - values[7 - a] for a in range(4)]
    result = None
    for table, part in zip(SQUARES, (sums, gaps)):
        for r in range(4):
            if table[r][r] == 0.0:
                continue
            term = table[r][r] * part[r]
            for c in range(r + 1, 4):
                term = term + table[r][c] * part[c]
            term = term * term
            result = term if result is None else result + term
    return result


def rows(start):
    return pl.ds(pl.multiple_of(start, 8), 8)


def every_eighth(start):
    return pl.ds(start, 8, stride=8)


def far_first(count):
    return sorted(range(1, count), key=lambda step: (abs(2 * step - count), step))


def sublane_sum(value):
    return jnp.sum(value, axis=0, keepdims=True)


def split(value):
    high = value.astype(jnp.bfloat16)
    low = (value - high.astype(jnp.float32)).astype(jnp.bfloat16)
    return high, low


def dot(first, second, dims):
    return lax.dot_general(
        first, second, (dims, ((), ())), preferred_element_type=jnp.float32
    )


def face_slice(face, base, step):
    direction, level = face // 2, 7 * (face % 2)
    if direction == 0:
        return pl.ds(pl.multiple_of(base + 64 * level + 8 * step, 8), 8)
    if direction == 1:
        return pl.ds(pl.multiple_of(base + 64 * step + 8 * level, 8), 8)
    return pl.ds(base + 64 * step + level, 8, stride=8)


def kernel(
    sizes,
    adjoint_hbm,
    velocity_hbm,
    geometry_hbm,
    codes_hbm,
    first,
    image,
    factor_ref,
    adjoint,
    velocity,
    geometry,
    codes,
    mass,
    along_i,
    along_k,
    columns,
    pairs,
    chosen,
    faces,
    gained,
    outgoing,
    incoming,
    partial,
    near_slots,
    far_slots,
    load_sem,
    face_send,
    face_recv,
    near_send,
    near_recv,
    far_send,
    far_recv,
):
    owners, n_y, n_z = sizes
    n_x = owners // 2
    me = lax.axis_index("sub")
    group = lax.axis_index("grp")
    my_y = group // n_z
    my_z = group - my_y * n_z
    my_x = me // 2
    my_core = me - my_x * 2

    def load(index, source, target):
        return pltpu.make_async_copy(source, target, load_sem.at[index])

    loads = [load(0, codes_hbm, codes), load(1, geometry_hbm, geometry)]
    loads.append(load(2, velocity_hbm, velocity))
    for index, (low, high) in enumerate(GROUPS):
        part = pl.ds(low * POINTS, (high - low) * POINTS)
        loads.append(load(3 + index, adjoint_hbm.at[part], adjoint.at[part]))
    for copy in loads:
        copy.start()

    barrier = pltpu.get_barrier_semaphore()
    n_near, n_far = 2 * n_z, n_x * n_y
    near_me = my_z * 2 + my_core
    far_me = my_y * n_x + my_x

    def sub_peer(step):
        return {"grp": group, "sub": lax.rem(me + step, owners)}

    def near_peer(step):
        place = lax.rem(near_me + step, n_near)
        z = place // 2
        return {"grp": my_y * n_z + z, "sub": my_x * 2 + (place - z * 2)}

    def far_peer(step):
        place = lax.rem(far_me + step, n_far)
        y = place // n_x
        return {"grp": y * n_z + my_z, "sub": (place - y * n_x) * 2 + my_core}

    for count, peer in ((owners, sub_peer), (n_near, near_peer), (n_far, far_peer)):

        def greet(step, carry, peer=peer):
            pl.semaphore_signal(barrier, inc=1, device_id=peer(step), device_id_type=MESH)
            return carry

        lax.fori_loop(1, count, greet, 0, unroll=4)

    sublane = lax.broadcasted_iota(jnp.int32, (8, 128), 0)
    lane = lax.broadcasted_iota(jnp.int32, (8, 128), 1).astype(jnp.float32)
    inside = jnp.where((sublane >= 1) & (sublane <= 6), 1.0, 0.0)
    depth_weight = jnp.zeros((8, 128), jnp.float32)
    for k in range(8):
        depth_weight = jnp.where(sublane == k, WEIGHTS[k], depth_weight)
    zero = jnp.zeros((8, 128), jnp.float32)

    loads[0].wait()
    for tile in range(6):
        width = min(128, 704 - 128 * tile)
        row = codes[:, 128 * tile : 128 * tile + width].astype(jnp.float32)
        columns[128 * tile : 128 * tile + width, :] = jnp.transpose(
            jnp.broadcast_to(row, (128, width))
        )
    lane16 = lax.broadcasted_iota(jnp.int32, (16, 128), 1).astype(jnp.float32)
    for block in range(owners):
        code = columns[2 * LPAIR + 16 * block : 2 * LPAIR + 16 * block + 16, :]
        for face in range(6):
            chosen[16 * block : 16 * block + 16, 128 * face : 128 * face + 128] = jnp.where(
                code == lane16 + float(128 * face), 1.0, 0.0
            ).astype(jnp.bfloat16)
    for index in range(len(GROUPS)):
        outgoing[0, index] = jnp.zeros((128, 128), jnp.float32)

    loads[1].wait()
    volume = jnp.broadcast_to(geometry[0:1, :], (8, 128))
    inverse = [jnp.broadcast_to(geometry[d : d + 1, :], (8, 128)) for d in range(1, 4)]
    squared = [value * value for value in inverse]
    weighted = volume * depth_weight
    for i in range(8):
        for j in range(8):
            mass[64 * i + 8 * j : 64 * i + 8 * j + 8, :] = weighted * (WEIGHTS[i] * WEIGHTS[j])
    loads[2].wait()

    def scale_velocity(index, carry):
        for d in range(3):
            place = rows(index * 8 + d * POINTS)
            velocity[place, :] = velocity[place, :] * inverse[d]
        return carry

    lax.fori_loop(0, 64, scale_velocity, 0, unroll=4)

    def build_pairs():
        def find(index, found):
            here = columns[rows(index * 8), :]
            there = columns[rows(index * 8 + LPAIR), :]
            result = []
            for face in range(6):
                place = lane + float(128 * face)
                value = jnp.where(here == place, there, found[face])
                result.append(jnp.where(there == place, here, value))
            return tuple(result)

        found = lax.fori_loop(0, LPAIR // 8, find, (zero - 1.0,) * 6, unroll=4)
        partner = [
            jnp.broadcast_to(jnp.max(value, axis=0, keepdims=True), (16, 128)) for value in found
        ]
        row_id = lax.broadcasted_iota(jnp.int32, (16, 128), 0).astype(jnp.float32)

        def mark(index, carry):
            place = row_id + (index * 16).astype(jnp.float32)
            here = pl.ds(pl.multiple_of(index * 16, 16), 16)
            for face in range(6):
                pairs[here, 128 * face : 128 * face + 128] = jnp.where(
                    partner[face] == place, 1.0, 0.0
                ).astype(jnp.bfloat16)
            return carry

        lax.fori_loop(0, 48, mark, 0, unroll=8)

    def sweep(source, base, table, factors, finish):
        def lines(r, carry):
            values = [source[rows(base + 64 * i + 8 * r), :] for i in range(8)]
            moved = product(values, table)
            for i in range(8):
                along_i[rows(64 * i + 8 * r), :] = (
                    values[i] * (1.0 / TIME_STEP) + factors(0, 64 * i + 8 * r) * moved[i]
                )
            values = [source[every_eighth(base + 64 * r + k), :] for k in range(8)]
            moved = product(values, table)
            for k in range(8):
                along_k[every_eighth(64 * r + k), :] = moved[k]
            return carry

        lax.fori_loop(0, 8, lines, 0, unroll=True)

        def close(i, carry):
            values = [source[rows(base + 64 * i + 8 * j), :] for j in range(8)]
            moved = product(values, table)
            for j in range(8):
                place = 64 * i + 8 * j
                total = along_i[rows(place), :] + factors(1, place) * moved[j]
                total = total + factors(2, place) * along_k[rows(place), :]
                carry = finish(place, values[j], mass[rows(place), :] * total, carry)
            return carry

        return lax.fori_loop(0, 8, close, (zero, zero), unroll=True)

    def note(quantity, comp, value):
        partial[pl.ds(quantity * 8 + comp, 1), :] = sublane_sum(value)

    def force(comp, carry):
        base = pl.multiple_of(comp * POINTS, POINTS)

        def finish(place, value, total, sums):
            first[rows(base + place), :] = total
            return sums[0] + total * total, sums[1]

        sums = sweep(
            adjoint,
            base,
            DERIVATIVE_HALVES,
            lambda d, place: velocity[rows(d * POINTS + place), :],
            finish,
        )
        note(0, comp, sums[0])
        return carry

    def kappas(comp):
        kappa = jnp.where(comp == 3, DIFFUSIVITY[3], DIFFUSIVITY[0])
        kappa = jnp.where(comp == 4, DIFFUSIVITY[4], kappa)
        return [kappa * value for value in squared]

    def spread(comp, carry):
        base = pl.multiple_of(comp * POINTS, POINTS)
        scaled = kappas(comp)

        def finish(place, value, total, sums):
            image[rows(base + place), :] = total
            return sums[0] + value * total, sums[1] + total * total

        sums = sweep(first, base, STIFFNESS_HALVES, lambda d, place: scaled[d], finish)
        note(1, comp, sums[0])
        note(2, comp, sums[1])
        return carry

    def energy(comp, carry):
        base = pl.multiple_of(comp * POINTS, POINTS)
        scaled = kappas(comp)
        forms = [zero, zero, zero]
        plain = zero
        for r in range(8):
            lines_i = [image[rows(base + 64 * i + 8 * r), :] for i in range(8)]
            forms[0] = forms[0] + WEIGHTS[r] * quadratic(lines_i)
            lines_j = [image[rows(base + 64 * r + 8 * j), :] for j in range(8)]
            forms[1] = forms[1] + WEIGHTS[r] * quadratic(lines_j)
            lines_k = [image[every_eighth(base + 64 * r + k), :] for k in range(8)]
            forms[2] = forms[2] + WEIGHTS[r] * quadratic(lines_k)
            level = [lines_j[j] * lines_j[j] for j in range(8)]
            level = sum((WEIGHTS[j] * (level[j] + level[7 - j]) for j in range(1, 4)), WEIGHTS[0] * (level[0] + level[7]))
            plain = plain + WEIGHTS[r] * level
        total = plain * (1.0 / TIME_STEP)
        for d in range(3):
            total = total + scaled[d] * forms[d]
        note(3, comp, weighted * total)
        return carry

    def face_copy(turn, index, step):
        peer = sub_peer(step)
        return pltpu.make_async_remote_copy(
            src_ref=outgoing.at[turn, index, pl.ds(pl.multiple_of(peer["sub"] * FMAX, FMAX), FMAX)],
            dst_ref=incoming.at[turn, index, pl.ds(pl.multiple_of(me * FMAX, FMAX), FMAX)],
            send_sem=face_send.at[turn, index, step],
            recv_sem=face_recv.at[turn, index, step],
            device_id=peer,
            device_id_type=MESH,
        )

    def each_copy(turn, index, act):
        for step in far_first(owners):
            act(face_copy(turn, index, step))

    def select(turn, index, field):
        low, high = GROUPS[index]

        def gather(comp, carry):
            base = pl.multiple_of(comp * POINTS, POINTS)
            top = pl.multiple_of(comp * FACE_ROWS, 16)
            for face in range(6):
                block = jnp.concatenate(
                    [field[face_slice(face, base, a), :] * inside for a in range(1, 7)], axis=0
                )
                big, small = split(block)
                place = slice(128 * face, 128 * face + 128)
                faces[pl.ds(top, FACE_ROWS), place] = big
                faces[pl.ds(pl.multiple_of(top + HALF_ROWS, 16), FACE_ROWS), place] = small
            return carry

        lax.fori_loop(low, high, gather, 0, unroll=True)
        start, stop = low * FACE_ROWS, high * FACE_ROWS
        over_lanes = ((1,), (1,))
        outgoing[turn, index, :, 0 : stop - start] = dot(
            chosen[...], faces[start:stop, :], over_lanes
        ) + dot(chosen[...], faces[HALF_ROWS + start : HALF_ROWS + stop, :], over_lanes)

    def start(turn, index):
        each_copy(turn, index, lambda copy: copy.start())

    plain_dims = ((1,), (0,))

    def local():
        for part in range(3):
            place = slice(256 * part, 256 * part + 256)
            gained[:, place] = dot(faces[0:HALF_ROWS, :], pairs[:, place], plain_dims) + dot(
                faces[HALF_ROWS:, :], pairs[:, place], plain_dims
            )

    def wait(turn, index):
        each_copy(turn, index, lambda copy: copy.wait_recv())

    def receive(turn, index, field, quantity):
        low, high = GROUPS[index]
        begin, stop = low * FACE_ROWS, high * FACE_ROWS
        big, small = split(jnp.transpose(incoming[turn, index])[0 : stop - begin, :])
        for part in range(3):
            place = slice(256 * part, 256 * part + 256)
            gained[begin:stop, place] = (
                gained[begin:stop, place]
                + dot(big, chosen[:, place], plain_dims)
                + dot(small, chosen[:, place], plain_dims)
            )

        def add(comp, carry):
            base = pl.multiple_of(comp * POINTS, POINTS)
            places = [face_slice(face, base, a + 1) for face in range(6) for a in range(6)]
            values = [field[place, :] for place in places]
            extra = [
                gained[rows(comp * FACE_ROWS + 8 * a), 128 * face : 128 * face + 128]
                for face in range(6)
                for a in range(6)
            ]
            sums = zero
            for place, value, more in zip(places, values, extra):
                sums = sums + value * more
                field[place, :] = value + more
            here = pl.ds(quantity * 8 + comp, 1)
            partial[here, :] = partial[here, :] + sublane_sum(sums)
            return carry

        lax.fori_loop(low, high, add, 0, unroll=True)

    faces[COMP * FACE_ROWS : HALF_ROWS, :] = jnp.zeros((16, 768), jnp.bfloat16)
    faces[HALF_ROWS + COMP * FACE_ROWS :, :] = jnp.zeros((16, 768), jnp.bfloat16)
    partial[...] = jnp.zeros((32, 128), jnp.float32)

    for index, (low, high) in enumerate(GROUPS):
        loads[3 + index].wait()
        lax.fori_loop(low, high, force, 0, unroll=True)
        select(0, index, first)
        if index == 0:
            pl.semaphore_wait(barrier, owners - 1 + n_near - 1 + n_far - 1)
        start(0, index)
    own = pl.ds(pl.multiple_of(me * FMAX, FMAX), FMAX)
    for index in range(len(GROUPS)):
        outgoing[1, index] = jnp.zeros((128, 128), jnp.float32)
        for turn in range(2):
            incoming[turn, index, own, :] = jnp.zeros((FMAX, 128), jnp.float32)
    build_pairs()
    local()
    last = len(GROUPS) - 1
    for index, (low, high) in enumerate(GROUPS):
        wait(0, index)
        if index > 0:
            select(1, index - 1, image)
        receive(0, index, first, 0)
        if index > 0:
            start(1, index - 1)
        lax.fori_loop(low, high, spread, 0, unroll=True)
    select(1, last, image)
    start(1, last)
    local()
    for index, (low, high) in enumerate(GROUPS):
        wait(1, index)
        receive(1, index, image, 2)
        lax.fori_loop(low, high, energy, 0, unroll=True)

    entry = lax.broadcasted_iota(jnp.int32, (32, 128), 0)
    column = lax.broadcasted_iota(jnp.int32, (32, 128), 1)
    diagonal = entry == column
    whole = jnp.sum(partial[...], axis=1, keepdims=True)
    row = jnp.sum(jnp.where(diagonal, whole, 0.0), axis=0, keepdims=True)

    def sum_copy(slots, mine, peer, send_sems, recv_sems, step):
        return pltpu.make_async_remote_copy(
            src_ref=slots.at[mine],
            dst_ref=slots.at[mine],
            send_sem=send_sems.at[step],
            recv_sem=recv_sems.at[step],
            device_id=peer(step),
            device_id_type=MESH,
        )

    stages = (
        (near_slots, n_near, near_me, near_peer, near_send, near_recv),
        (far_slots, n_far, far_me, far_peer, far_send, far_recv),
    )
    for slots, count, mine, peer, send_sems, recv_sems in stages:
        slots[mine] = row

        for step in far_first(count):
            sum_copy(slots, mine, peer, send_sems, recv_sems, step).start()
        if slots is near_slots:
            for turn in range(2):
                for index in range(len(GROUPS)):
                    each_copy(turn, index, lambda copy: copy.wait_send())
        for step in far_first(count):
            sum_copy(slots, mine, peer, send_sems, recv_sems, step).wait_send()
        for step in reversed(far_first(count)):
            sum_copy(slots, mine, peer, send_sems, recv_sems, step).wait_recv()
        row = jnp.sum(slots[...], axis=0)

    spreaded = jnp.where(diagonal, jnp.broadcast_to(row, (32, 128)), 0.0)
    totals = jnp.broadcast_to(jnp.sum(spreaded, axis=1, keepdims=True), (32, 128))
    bb, bq, qq, qhq = (totals[8 * n : 8 * n + 8] for n in range(4))
    alpha = bb / bq
    scaled_qq = alpha * qq
    norm_next = alpha * scaled_qq - bb
    beta = norm_next / bb
    up = 1.0 + beta
    curve = up * (up * bq - 2.0 * scaled_qq) + alpha * (alpha * qhq)
    alpha_next = norm_next / curve
    factor_ref[0:8, :] = alpha + alpha_next * up
    factor_ref[8:16, :] = -alpha * alpha_next


def solution(mesh):
    owners, groups = mesh.shape["sub"], mesh.shape["grp"]
    n_z = 12 if groups % 12 == 0 else max(1, groups // 2)
    n_y = groups // n_z

    def shards(adjoint, velocity, geometry, face_codes):
        elements = adjoint.shape[2]
        flat = COMP * POINTS
        vmem = pltpu.VMEM
        f32, bf16 = jnp.float32, jnp.bfloat16
        hbm = pl.BlockSpec(memory_space=pltpu.HBM)

        def keep(array):
            return pltpu.with_memory_space_constraint(array, pltpu.HBM)

        inner = pl.BlockSpec(memory_space=pltpu.VMEM)
        n_near, n_far = 2 * n_z, n_y * owners // 2
        dma = pltpu.SemaphoreType.DMA
        first, image, factor = pl.pallas_call(
            functools.partial(kernel, (owners, n_y, n_z)),
            out_shape=(
                pltpu.VMEM((flat, elements), f32),
                pltpu.VMEM((flat, elements), f32),
                pltpu.VMEM((16, elements), f32),
            ),
            in_specs=[hbm] * 4,
            out_specs=(inner, inner, inner),
            scratch_shapes=[
                vmem((flat, elements), f32),
                vmem((3 * POINTS, elements), f32),
                vmem((4, elements), f32),
                vmem((1, 704), jnp.int32),
                vmem((POINTS, elements), f32),
                vmem((POINTS, elements), f32),
                vmem((POINTS, elements), f32),
                vmem((704, 128), f32),
                vmem((768, 768), bf16),
                vmem((128, 768), bf16),
                vmem((2 * HALF_ROWS, 768), bf16),
                vmem((HALF_ROWS, 768), f32),
                vmem((2, len(GROUPS), 128, 128), f32),
                vmem((2, len(GROUPS), 128, 128), f32),
                vmem((32, 128), f32),
                vmem((n_near, 1, 128), f32),
                vmem((n_far, 1, 128), f32),
                dma((3 + len(GROUPS),)),
                dma((2, len(GROUPS), owners)),
                dma((2, len(GROUPS), owners)),
                dma((n_near,)),
                dma((n_near,)),
                dma((n_far,)),
                dma((n_far,)),
            ],
            compiler_params=pltpu.CompilerParams(
                collective_id=0, has_side_effects=True, vmem_limit_bytes=32 * 1024 * 1024
            ),
        )(
            keep(adjoint.reshape(flat, elements)),
            keep(velocity.reshape(3 * POINTS, elements)),
            keep(geometry),
            keep(face_codes),
        )
        shape = (COMP, POINTS, elements)
        return (
            factor[0:COMP, None, :] * first.reshape(shape)
            + factor[8 : 8 + COMP, None, :] * image.reshape(shape)
        )

    placed = (
        P(None, None, ("grp", "sub")),
        P(None, None, ("grp", "sub")),
        P(None, ("grp", "sub")),
        P(("grp", "sub"), None),
    )
    return jax.shard_map(
        shards, mesh=mesh, in_specs=placed, out_specs=P(None, None, ("grp", "sub")), check_vma=False
    )
```
